32 devices in a mesh: dp: 4 (over y, x), ctx: 8 (over z, core).
Axes of the slice: x: 2, y: 2, z: 4, core: 2. Of those that a mesh axis runs over, the one named last changes fastest.
Arguments:
- tokens: bfloat16 [8, 2048, 2048], P('dp', 'ctx'), may hold values from -6 to 6
- output_grad: bfloat16 [8, 2048, 2048], P('dp', 'ctx'), may hold values from -6 to 6
- segment_ids: int32 [8, 2048], P('dp', 'ctx'), may hold values from 0 to 3, as said below
- positions: int32 [8, 2048], P('dp', 'ctx'), may hold values from 0 to 4095, as said below
- qkv_weight: float32 [2048, 3072], P(('dp', 'ctx')), may hold values from -0.125 to 0.125
- qkv_first: float32 [2048, 3072], P(('dp', 'ctx')), may hold values from -96 to 96
- qkv_second: float32 [2048, 3072], P(('dp', 'ctx')), may hold values from 1185.6842 to 4742.737
- out_weight: float32 [2048, 2048], P(('dp', 'ctx')), may hold values from -1 to 1
- out_first: float32 [2048, 2048], P(('dp', 'ctx')), may hold values from -6 to 6
- out_second: float32 [2048, 2048], P(('dp', 'ctx')), may hold values from 5.4325895 to 21.730358
- gate_up_weight: float32 [2048, 16384], P(('dp', 'ctx')), may hold values from -0.125 to 0.125
- gate_up_first: float32 [2048, 16384], P(('dp', 'ctx')), may hold values from -24 to 24
- gate_up_second: float32 [2048, 16384], P(('dp', 'ctx')), may hold values from 77.60842 to 310.4337
- down_weight: float32 [8192, 2048], P(('dp', 'ctx')), may hold values from -0.0625 to 0.0625
- down_first: float32 [8192, 2048], P(('dp', 'ctx')), may hold values from -48 to 48
- down_second: float32 [8192, 2048], P(('dp', 'ctx')), may hold values from 310.4337 to 1241.7347
- norm_gains: float32 [2, 2048], P(None, ('dp', 'ctx')), may hold values from 0.5 to 1.5
- norm_first: float32 [2, 2048], P(None, ('dp', 'ctx')), may hold values from -96 to 96
- norm_second: float32 [2, 2048], P(None, ('dp', 'ctx')), may hold values from 1185.6842 to 4742.737
- head_gains: float32 [2, 64], replicated, may hold values from 0.5 to 1.5
- head_first: float32 [2, 64], replicated, may hold values from -256 to 256
- head_second: float32 [2, 64], replicated, may hold values from 9485.474 to 37941.895
Outputs:
- outputs: bfloat16 [8, 2048, 2048], P('dp', 'ctx')
- input_grad: bfloat16 [8, 2048, 2048], P('dp', 'ctx')
- new_qkv: float32 [2048, 3072], P(('dp', 'ctx'))
- new_qkv_first: float32 [2048, 3072], P(('dp', 'ctx'))
- new_qkv_second: float32 [2048, 3072], P(('dp', 'ctx'))
- new_out: float32 [2048, 2048], P(('dp', 'ctx'))
- new_out_first: float32 [2048, 2048], P(('dp', 'ctx'))
- new_out_second: float32 [2048, 2048], P(('dp', 'ctx'))
- new_gate_up: float32 [2048, 16384], P(('dp', 'ctx'))
- new_gate_up_first: float32 [2048, 16384], P(('dp', 'ctx'))
- new_gate_up_second: float32 [2048, 16384], P(('dp', 'ctx'))
- new_down: float32 [8192, 2048], P(('dp', 'ctx'))
- new_down_first: float32 [8192, 2048], P(('dp', 'ctx'))
- new_down_second: float32 [8192, 2048], P(('dp', 'ctx'))
- new_norm_gains: float32 [2, 2048], P(None, ('dp', 'ctx'))
- new_norm_first: float32 [2, 2048], P(None, ('dp', 'ctx'))
- new_norm_second: float32 [2, 2048], P(None, ('dp', 'ctx'))
- new_head_gains: float32 [2, 64], replicated
- new_head_first: float32 [2, 64], replicated
- new_head_second: float32 [2, 64], replicated
The draws below stay inside these ranges and needn't reach their ends.
Inputs may be any that keep to these rules, and one draw needn't show every extreme that they name: `segment_ids`: within each sequence the ids start at 0 and never fall by more than nothing; documents other than a sequence's last hold 204 tokens or more; in each dp index one of its 2 sequences is a single document, and every other sequence holds 4 documents, the first three of 512 tokens at most. `positions`: positions count up by one within a document from 0, except that a sequence's first document may start at a later position.
All inputs are finite; a program needn't handle non-finite values.
Results may differ from the reference program's by a relative error of at most 0.04.
Values may be sent and summed in bfloat16 or wider, within the bound.
A program may use at most 408 MiB of HBM per device.

```python
import math
import jax
import jax.numpy as jnp
from jax import lax

D = 2048
H = 32
KV = 8
HD = 64
FF = 8192
SEQ_LEN = 2048
SEQS = 2
STEP = 5
NSEQ = 8
TOKENS = 16384
N_DP = 4


def document_layout(key):
    key_lengths, key_whole, key_offset, key_head = jax.random.split(key, 4)
    shortest = SEQ_LEN // 10
    longest = SEQ_LEN * 15 // 16
    doc_slots = SEQ_LEN // shortest + 1
    lengths = jax.random.randint(key_lengths, (NSEQ, doc_slots), shortest, longest + 1)
    head_lengths = jax.random.randint(key_head, (NSEQ, 3), shortest, SEQ_LEN // 4 + 1)
    lengths = jnp.concatenate([head_lengths, lengths[:, 3:]], axis=1)
    doc_ends = jnp.cumsum(lengths, axis=1).astype(jnp.int32)
    places = jnp.arange(SEQ_LEN).astype(jnp.int32)
    segments = jnp.sum((doc_ends[:, None, :] <= places[None, :, None]).astype(jnp.int32), axis=2)
    segments = jnp.minimum(segments, 3)
    chosen = jax.random.randint(key_whole, (N_DP,), 0, SEQS)
    whole_doc = jnp.arange(NSEQ) % SEQS == jnp.repeat(chosen, SEQS)
    segments = jnp.where(whole_doc[:, None], 0, segments).astype(jnp.int32)
    starts = jnp.concatenate([jnp.zeros((NSEQ, 1), jnp.int32), doc_ends[:, :-1]], axis=1)
    doc_begin = jnp.take_along_axis(starts, segments, axis=1)
    offset = jax.random.randint(key_offset, (NSEQ, 1), 0, SEQ_LEN)
    group_rank = (jnp.arange(NSEQ) // SEQS)[:, None]
    offset = jnp.where(whole_doc[:, None] & (group_rank == 0), SEQ_LEN, offset)
    offset = jnp.where(whole_doc[:, None] & (group_rank == 1), 0, offset)
    place_ids = places[None, :] - doc_begin + jnp.where(segments == 0, offset, 0)
    return (segments, place_ids.astype(jnp.int32))


def draw_segment_ids(key, part):
    segments, place_ids = document_layout(key)
    return segments


def draw_positions(key, part):
    segments, place_ids = document_layout(key)
    return place_ids


def block_levels(key, shape, cuts, smallest, high):
    loudness = 1.0
    for dim, blocks in cuts:
        draws = jax.random.uniform(jax.random.fold_in(jax.random.fold_in(key, 6), dim), (blocks,), jnp.float32, smallest / len(cuts), high / len(cuts))
        loudness = loudness * jnp.repeat(jnp.exp(draws), shape[dim] // blocks).reshape((-1,) + (1,) * (len(shape) - 1 - dim))
    return loudness


def normal_values(key, dims, spread, most, cuts=(), kind=jnp.bfloat16):
    entries = spread * jax.random.normal(key, dims, jnp.float32)
    if cuts:
        entries = entries * block_levels(key, dims, cuts, -0.22, 0.18)
    return jnp.clip(entries, -most, most).astype(kind)


def setup_inputs(seed: int = 0) -> dict:
    keys = jax.random.split(jax.random.key(seed), 23)
    return {
        "tokens": normal_values(keys[0], (NSEQ, SEQ_LEN, D), 1.0, 6.0, ((0, 4), (1, 8))),
        "output_grad": normal_values(keys[1], (NSEQ, SEQ_LEN, D), 1.0, 6.0, ((0, 4), (1, 8))),
        "segment_ids": draw_segment_ids(jax.random.fold_in(keys[22], 71), 0),
        "positions": draw_positions(jax.random.fold_in(keys[22], 71), 0),
        "qkv_weight": normal_values(keys[4], (D, (H + 2 * KV) * HD), D ** -0.5, 0.125, ((0, 32),), jnp.float32),
        "qkv_first": normal_values(keys[5], (D, (H + 2 * KV) * HD), ((TOKENS * (1 + 768 / SEQ_LEN)) ** 0.5 / 9), 96.0, ((0, 32),), jnp.float32),
        "qkv_second": jnp.clip(jnp.exp(math.log(4742.737) - 1.3862944 * jax.random.uniform(keys[6], (D, (H + 2 * KV) * HD), jnp.float32) ** block_levels(keys[6], (D, (H + 2 * KV) * HD), ((0, 32),), -0.2, 0.2)), 1185.6842, 4742.737),
        "out_weight": normal_values(keys[7], (H * HD, D), (D // 64) ** -0.5, 1.0, ((0, 32),), jnp.float32),
        "out_first": normal_values(keys[8], (H * HD, D), (0.0067 * (TOKENS * (1 + 1536 / SEQ_LEN)) ** 0.5), 6.0, ((0, 32),), jnp.float32),
        "out_second": jnp.clip(jnp.exp(math.log(21.730358) - 1.3862944 * jax.random.uniform(keys[9], (H * HD, D), jnp.float32) ** block_levels(keys[9], (H * HD, D), ((0, 32),), -0.2, 0.2)), 5.4325895, 21.730358),
        "gate_up_weight": normal_values(keys[10], (D, 2 * FF), D ** -0.5, 0.125, ((0, 32),), jnp.float32),
        "gate_up_first": normal_values(keys[11], (D, 2 * FF), (0.033 * TOKENS ** 0.5), 24.0, ((0, 32),), jnp.float32),
        "gate_up_second": jnp.clip(jnp.exp(math.log(310.4337) - 1.3862944 * jax.random.uniform(keys[12], (D, 2 * FF), jnp.float32) ** block_levels(keys[12], (D, 2 * FF), ((0, 32),), -0.2, 0.2)), 77.60842, 310.4337),
        "down_weight": normal_values(keys[13], (FF, D), FF ** -0.5, 0.0625, ((0, 32),), jnp.float32),
        "down_first": normal_values(keys[14], (FF, D), (0.067 * TOKENS ** 0.5), 48.0, ((0, 32),), jnp.float32),
        "down_second": jnp.clip(jnp.exp(math.log(1241.7347) - 1.3862944 * jax.random.uniform(keys[15], (FF, D), jnp.float32) ** block_levels(keys[15], (FF, D), ((0, 32),), -0.2, 0.2)), 310.4337, 1241.7347),
        "norm_gains": jnp.clip(1.0 + 0.1 * jax.random.normal(keys[16], (2, D), jnp.float32), 0.5, 1.5),
        "norm_first": normal_values(keys[17], (2, D), ((TOKENS * (1 + 768 / SEQ_LEN)) ** 0.5 / 9), 96.0, ((1, 32),), jnp.float32),
        "norm_second": jnp.clip(jnp.exp(math.log(4742.737) - 1.3862944 * jax.random.uniform(keys[18], (2, D), jnp.float32) ** block_levels(keys[18], (2, D), ((1, 32),), -0.2, 0.2)), 1185.6842, 4742.737),
        "head_gains": jnp.clip(1.0 + 0.1 * jax.random.normal(keys[19], (2, HD), jnp.float32), 0.5, 1.5),
        "head_first": normal_values(keys[20], (2, HD), (0.056 * (TOKENS * H * (1 + 768 / SEQ_LEN)) ** 0.5), 256.0, (), jnp.float32),
        "head_second": jnp.clip(jnp.exp(jax.random.uniform(keys[21], (2, HD), jnp.float32, math.log(9485.474), math.log(37941.895))), 9485.474, 37941.895),
    }


EPS = 1e-05
ROPE_BASE = 1000000.0
BETA_ONE = 0.9
BETA_TWO = 0.95
ADAM_EPS = 1e-08
DECAY = 0.1
RATE_QKV = 0.05
RATE_OUT = 0.3
RATE_GATE_UP = 0.05
RATE_DOWN = 0.03
RATE_GAIN = 0.5
HIGHEST = lax.Precision.HIGHEST

@jax.custom_vjp
def low(v):
    return lax.optimization_barrier(v.astype(jnp.bfloat16)).astype(jnp.float32)

@jax.custom_vjp
def low_back(v):
    return v

def low_keep(v):
    return (low(v), None)

def low_pass(kept, grad):
    return (grad,)

def back_keep(v):
    return (v, None)

def back_low(kept, grad):
    return (low(grad),)
low.defvjp(low_keep, low_pass)
low_back.defvjp(back_keep, back_low)

def product(left, right):
    return jnp.dot(left, right, precision=HIGHEST)

def rms_norm(values, gain):
    return values * lax.rsqrt(lax.optimization_barrier(jnp.mean(values * values, axis=-1, keepdims=True)) + EPS) * gain

def rotary(values, cosine, sine_table):
    half_width = values.shape[-1] // 2
    first_half = values[..., :half_width]
    second_half = values[..., half_width:]
    return jnp.concatenate([first_half * cosine - second_half * sine_table, second_half * cosine + first_half * sine_table], axis=-1)

def rotary_tables(place_ids):
    freqs = ROPE_BASE ** (-(jnp.arange(HD // 2).astype(jnp.float32) * 2.0 / HD))
    angles = place_ids.astype(jnp.float32)[..., None] * freqs
    return (jnp.cos(angles), jnp.sin(angles))

def sequence_block(weights, row_inputs):
    qkv_matrix, out_matrix, gate_up_matrix, down_matrix, norm_gain, head_gain = weights
    inputs, segments, place_ids = row_inputs
    group_size = H // KV
    normed = low(rms_norm(inputs, norm_gain[0]))
    projected = low_back(product(normed, qkv_matrix))
    query_raw = projected[:, :H * HD].reshape(SEQ_LEN, KV, group_size, HD)
    keys_raw = projected[:, H * HD:(H + KV) * HD].reshape(SEQ_LEN, KV, HD)
    value_rows = low(projected[:, (H + KV) * HD:].reshape(SEQ_LEN, KV, HD))
    cosine, sine_table = rotary_tables(place_ids)
    query_rot = low(rotary(rms_norm(query_raw, head_gain[0]), cosine[:, None, None, :], sine_table[:, None, None, :]))
    keys_rot = low(rotary(rms_norm(keys_raw, head_gain[1]), cosine[:, None, :], sine_table[:, None, :]))
    index_rows = jnp.arange(SEQ_LEN)
    allowed = (index_rows[None, :] <= index_rows[:, None]) & (segments[None, :] == segments[:, None])

    def attend(item_row):
        query_group, key_head, value_head = item_row
        scores = low_back(jnp.einsum('qgd,kd->gqk', query_group, key_head, precision=HIGHEST) * HD ** (-0.5))
        scores = jnp.where(allowed[None], scores, -1e+30)
        row_max = lax.optimization_barrier(jnp.max(scores, axis=-1, keepdims=True))
        exp_scores = jnp.exp(scores - row_max)
        probs = low(exp_scores / lax.optimization_barrier(jnp.sum(exp_scores, axis=-1, keepdims=True)))
        return jnp.einsum('gqk,kd->qgd', probs, value_head, precision=HIGHEST)
    heads = lax.map(jax.checkpoint(attend), (query_rot.transpose(1, 0, 2, 3), keys_rot.transpose(1, 0, 2), value_rows.transpose(1, 0, 2)))
    attended = low(low_back(heads.transpose(1, 0, 2, 3).reshape(SEQ_LEN, H * HD)))
    middle = inputs + low_back(product(attended, out_matrix))
    feed_in = low(rms_norm(middle, norm_gain[1]))
    gate_up = low_back(product(feed_in, gate_up_matrix))
    hidden = low(jax.nn.silu(gate_up[:, :FF]) * gate_up[:, FF:])
    return middle + low_back(product(hidden, down_matrix))

def adam(master, moment_one, moment_two, grad_in, step_rate, decay_rate):
    first_new = BETA_ONE * moment_one + (1.0 - BETA_ONE) * grad_in
    second_new = BETA_TWO * moment_two + (1.0 - BETA_TWO) * grad_in * grad_in
    first_hat = first_new / (1.0 - BETA_ONE ** STEP)
    second_hat = second_new / (1.0 - BETA_TWO ** STEP)
    master_new = master - step_rate * (first_hat / (jnp.sqrt(second_hat) + ADAM_EPS) + decay_rate * master)
    return (master_new, first_new, second_new)

def reference(tokens, output_grad, segment_ids, positions, qkv_weight, qkv_first, qkv_second, out_weight, out_first, out_second, gate_up_weight, gate_up_first, gate_up_second, down_weight, down_first, down_second, norm_gains, norm_first, norm_second, head_gains, head_first, head_second):
    masters = (qkv_weight, out_weight, gate_up_weight, down_weight, norm_gains, head_gains)

    def layer(params, inputs):
        rounded = tuple((low(matrix) for matrix in params[:4])) + tuple(params[4:])

        def one_sequence(row_inputs):
            return sequence_block(rounded, row_inputs)
        return lax.map(jax.checkpoint(one_sequence), (inputs, segment_ids, positions))
    results, pullback = jax.vjp(layer, masters, tokens.astype(jnp.float32))
    grads, input_grad = pullback(output_grad.astype(jnp.float32))
    qkv_new = adam(qkv_weight, qkv_first, qkv_second, grads[0], RATE_QKV, DECAY)
    out_new = adam(out_weight, out_first, out_second, grads[1], RATE_OUT, DECAY)
    gate_up_new = adam(gate_up_weight, gate_up_first, gate_up_second, grads[2], RATE_GATE_UP, DECAY)
    down_new = adam(down_weight, down_first, down_second, grads[3], RATE_DOWN, DECAY)
    norm_new = adam(norm_gains, norm_first, norm_second, grads[4], RATE_GAIN, 0.0)
    head_new = adam(head_gains, head_first, head_second, grads[5], RATE_GAIN, 0.0)
    return (results.astype(jnp.bfloat16), input_grad.astype(jnp.bfloat16), qkv_new[0], qkv_new[1], qkv_new[2], out_new[0], out_new[1], out_new[2], gate_up_new[0], gate_up_new[1], gate_up_new[2], down_new[0], down_new[1], down_new[2], norm_new[0], norm_new[1], norm_new[2], head_new[0], head_new[1], head_new[2])
```

```python
import functools
import math

import jax
import jax.numpy as jnp
from jax import lax
from jax.experimental import pallas as pl
from jax.experimental.pallas import tpu as pltpu
from jax.sharding import PartitionSpec as P

H = 32
KV = 8
HD = 64
G = H // KV
STEP = 5

EPS = 1e-05
ROPE_BASE = 1000000.0
BETA_ONE = 0.9
BETA_TWO = 0.95
ADAM_EPS = 1e-08
DECAY = 0.1
RATE_QKV = 0.05
RATE_OUT = 0.3
RATE_GATE_UP = 0.05
RATE_DOWN = 0.03
RATE_GAIN = 0.5

LOW = jnp.bfloat16
F32 = jnp.float32


def rms_scale(values):
    return lax.rsqrt(jnp.mean(values * values, axis=-1, keepdims=True) + EPS)


def norm_back(scaled, values, inv_rms):
    inner = jnp.mean(scaled * values, axis=-1, keepdims=True)
    return inv_rms * (scaled - values * inv_rms * inv_rms * inner)


def rotary(values, cosine, sine):
    first, second = values[..., : HD // 2], values[..., HD // 2 :]
    return jnp.concatenate([first * cosine - second * sine, second * cosine + first * sine], axis=-1)


def rotary_back(grad, cosine, sine):
    first, second = grad[..., : HD // 2], grad[..., HD // 2 :]
    return jnp.concatenate([first * cosine + second * sine, second * cosine - first * sine], axis=-1)


def rotary_tables(place_ids):
    freqs = ROPE_BASE ** (-(jnp.arange(HD // 2).astype(F32) * 2.0 / HD))
    angles = place_ids.astype(F32)[..., None] * freqs
    return (jnp.cos(angles), jnp.sin(angles))


def dot(left, right, dims):
    return lax.dot_general(left, right, (dims, ((), ())), preferred_element_type=F32)


NN = ((1,), (0,))
NT = ((1,), (1,))
TN = ((0,), (0,))


def adam(master, moment_one, moment_two, grad, step_rate, decay_rate):
    first_new = BETA_ONE * moment_one + (1.0 - BETA_ONE) * grad
    second_new = BETA_TWO * moment_two + (1.0 - BETA_TWO) * grad * grad
    first_hat = first_new / (1.0 - BETA_ONE**STEP)
    second_hat = second_new / (1.0 - BETA_TWO**STEP)
    master_new = master - step_rate * (
        first_hat / (jnp.sqrt(second_hat) + ADAM_EPS) + decay_rate * master
    )
    return (master_new, first_new, second_new)


def chunk_mask(chunk, length, start, query_index):
    key_index = chunk * length + lax.broadcasted_iota(jnp.int32, (length, start.shape[1]), 0)
    return (key_index >= start) & (key_index <= query_index)


def for_chunks(meta_ref, step):
    place, low, full = meta_ref[0], meta_ref[1], meta_ref[2]

    @pl.loop(low, full)
    def _(chunk):
        step(chunk, True)

    @pl.loop(full, place)
    def _(chunk):
        step(chunk, False)

    step(place, True)


def attend_kernel(turned, meta_ref, start_ref, index_ref, query_ref, kv_ref, out_ref, log_ref, acc_ref):
    length = query_ref.shape[1] // G
    start, query_index = start_ref[...], index_ref[...]
    lane = lax.broadcasted_iota(jnp.int32, (length, 2 * HD), 1)
    acc_ref[...] = jnp.zeros_like(acc_ref)

    def step(chunk, masked):
        slot = kv_ref.shape[0] - 1 - chunk if turned else chunk
        kv = kv_ref[slot, 0]
        ones_v = jnp.where(lane < HD, jnp.ones_like(kv), kv)
        probs = jnp.exp(dot(kv, query_ref[0], NT))
        if masked:
            probs = jnp.where(chunk_mask(chunk, length, start, query_index), probs, 0.0)
        acc_ref[...] += dot(ones_v, probs.astype(LOW), TN)

    for_chunks(meta_ref, step)
    total = acc_ref[:1, :]
    log_ref[0] = jnp.log(total)
    mixed = acc_ref[HD:, :] / total
    rows = [mixed[:, head * length : (head + 1) * length] for head in range(G)]
    out_ref[...] = jnp.concatenate(rows, axis=0).T.astype(out_ref.dtype)


def attend_back_kernel(
    turned,
    meta_ref,
    start_ref,
    index_ref,
    query_ref,
    kv_ref,
    grad_ref,
    log_ref,
    inner_ref,
    dq_ref,
    dkv_ref,
    acc_ref,
):
    length = query_ref.shape[1] // G
    start, query_index = start_ref[...], index_ref[...]
    acc_ref[...] = jnp.zeros_like(acc_ref)
    dkv_ref[...] = jnp.zeros_like(dkv_ref)

    def step(chunk, masked):
        slot = kv_ref.shape[0] - 1 - chunk if turned else chunk
        kv = kv_ref[slot, 0]
        total = jnp.zeros((length, 2 * HD), F32)
        for head in range(G):
            part = pl.ds(head * length, length)
            query, grad = query_ref[0, part], grad_ref[0, part]
            probs = jnp.exp(dot(kv, query, NT) - log_ref[0, :, part])
            if masked:
                mask = chunk_mask(chunk, length, start[:, :length], query_index[:, :length])
                probs = jnp.where(mask, probs, 0.0)
            d_probs = dot(kv, grad, NT)
            d_scores = (probs * (d_probs - inner_ref[0, :, part])).astype(LOW)
            total = total + dot(d_scores, query, NN) + dot(probs.astype(LOW), grad, NN)
            acc_ref[:, part] += dot(kv, d_scores, TN)
        dkv_ref[slot, 0] = total.astype(dkv_ref.dtype)

    for_chunks(meta_ref, step)
    rows = [acc_ref[:HD, head * length : (head + 1) * length] for head in range(G)]
    dq_ref[...] = jnp.concatenate(rows, axis=0).T * (1.0 / math.sqrt(HD))


def attention_specs(n_ctx, length):
    query = pl.BlockSpec((1, G * length, 2 * HD), lambda h, *_: (h, 0, 0))
    kv = pl.BlockSpec((n_ctx, 1, length, 2 * HD), lambda h, *_: (0, h, 0, 0))
    row = pl.BlockSpec((1, 1, G * length), lambda h, *_: (h, 0, 0))
    start = pl.BlockSpec((1, G * length), lambda h, *_: (0, 0))
    natural = pl.BlockSpec((length, G * HD), lambda h, *_: (0, h))
    return query, kv, row, start, natural


def attend(turned, meta, start, index, query, kv_all):
    n_ctx, heads, length, _ = kv_all.shape
    q_spec, kv_spec, row_spec, start_spec, natural = attention_specs(n_ctx, length)
    pairs = heads * G * length * n_ctx * length
    return pl.pallas_call(
        functools.partial(attend_kernel, turned),
        grid_spec=pltpu.PrefetchScalarGridSpec(
            num_scalar_prefetch=1,
            grid=(heads,),
            in_specs=[start_spec, start_spec, q_spec, kv_spec],
            out_specs=[natural, row_spec],
            scratch_shapes=[pltpu.VMEM((2 * HD, G * length), F32)],
        ),
        out_shape=[
            jax.ShapeDtypeStruct((length, heads * G * HD), LOW),
            jax.ShapeDtypeStruct((heads, 1, G * length), F32),
        ],
        compiler_params=pltpu.CompilerParams(vmem_limit_bytes=40 * 2**20),
        cost_estimate=pl.CostEstimate(
            flops=pairs * 512, bytes_accessed=16 * 2**20, transcendentals=pairs
        ),
        name="attend",
    )(meta, start, index, query, kv_all)


def attend_back(turned, meta, start, index, query, kv_all, grad, log_total, inner):
    n_ctx, heads, length, _ = kv_all.shape
    q_spec, kv_spec, row_spec, start_spec, natural = attention_specs(n_ctx, length)
    pairs = heads * G * length * n_ctx * length
    return pl.pallas_call(
        functools.partial(attend_back_kernel, turned),
        grid_spec=pltpu.PrefetchScalarGridSpec(
            num_scalar_prefetch=1,
            grid=(heads,),
            in_specs=[start_spec, start_spec, q_spec, kv_spec, q_spec, row_spec, row_spec],
            out_specs=[natural, kv_spec],
            scratch_shapes=[pltpu.VMEM((2 * HD, G * length), F32)],
        ),
        out_shape=[
            jax.ShapeDtypeStruct((length, heads * G * HD), F32),
            jax.ShapeDtypeStruct(kv_all.shape, LOW),
        ],
        compiler_params=pltpu.CompilerParams(vmem_limit_bytes=40 * 2**20),
        cost_estimate=pl.CostEstimate(
            flops=pairs * 1280, bytes_accessed=32 * 2**20, transcendentals=pairs
        ),
        name="attend_back",
    )(meta, start, index, query, kv_all, grad, log_total, inner)


def partners(values, axis, shift):
    count = lax.axis_size(axis)
    return lax.ppermute(values, axis, [(i, i ^ shift) for i in range(count)])


def gather_dp(values):
    count = lax.axis_size("dp")
    return [values] + [partners(values, "dp", shift) for shift in range(1, count)]


def reduce_dp(blocks):
    total = blocks[0].astype(F32)
    for shift in range(1, len(blocks)):
        total = total + partners(blocks[shift].astype(LOW), "dp", shift).astype(F32)
    return total


def exchange(blocks, axis):
    count = blocks.shape[0]
    rank = lax.axis_index(axis)
    own = lax.dynamic_index_in_dim(blocks, rank, 0, keepdims=True)
    result = lax.dynamic_update_slice_in_dim(jnp.zeros_like(blocks), own, rank, 0)
    for shift in range(1, count):
        block = lax.dynamic_index_in_dim(blocks, rank ^ shift, 0, keepdims=True)
        block = partners(block, axis, shift)
        result = lax.dynamic_update_slice_in_dim(result, block, rank ^ shift, 0)
    return result


def mirror(values):
    count = lax.axis_size("ctx")
    return lax.ppermute(values, "ctx", [(i, count - 1 - i) for i in range(count)])


def body(
    tokens,
    output_grad,
    segment_ids,
    positions,
    qkv_weight,
    qkv_first,
    qkv_second,
    out_weight,
    out_first,
    out_second,
    gate_up_weight,
    gate_up_first,
    gate_up_second,
    down_weight,
    down_first,
    down_second,
    norm_gains,
    norm_first,
    norm_second,
    head_gains,
    head_first,
    head_second,
):
    n_dp, n_ctx = lax.axis_size("dp"), lax.axis_size("ctx")
    ctx_rank = lax.axis_index("ctx")
    seqs, length, width = tokens.shape
    own = norm_gains.shape[1]
    ff = down_weight.shape[0] * n_dp * n_ctx
    part = ff // n_dp
    everyone = ("dp", "ctx")

    gain_one, gain_two = norm_gains[0][:, None], norm_gains[1][:, None]
    qkv_low = qkv_weight.astype(LOW).astype(F32)
    gate_up_low = gate_up_weight.astype(LOW).astype(F32)
    qkv_full = lax.all_gather((qkv_low * gain_one).astype(LOW), everyone, axis=0, tiled=True)
    gate_up_blocks = (
        (gate_up_low * gain_two).astype(LOW).reshape(own, 2, n_dp, part).transpose(2, 0, 1, 3)
    )
    gate_up_mine = exchange(gate_up_blocks.reshape(n_dp, own, 2 * part), "dp")
    gate_up_part = lax.all_gather(
        gate_up_mine.reshape(n_dp * own, 2 * part), "ctx", axis=0, tiled=True
    )
    down_part = lax.all_gather(down_weight.astype(LOW), "ctx", axis=0, tiled=True)
    out_full = lax.all_gather(out_weight.astype(LOW), everyone, axis=0, tiled=True)

    places = jnp.stack([segment_ids, positions], axis=1)
    tokens_of, grads_of, places_of, rank_of = [], [], [], []
    for seq in range(seqs):
        turned = seq % 2 == 1
        tokens_of.append(mirror(tokens[seq]) if turned else tokens[seq])
        grads_of.append(mirror(output_grad[seq]) if turned else output_grad[seq])
        places_of.append(mirror(places[seq]) if turned else places[seq])
        rank_of.append(n_ctx - 1 - ctx_rank if turned else ctx_rank)

    def project(seq):
        inputs = tokens_of[seq].astype(F32)
        scale_one = rms_scale(inputs)
        normed = (inputs * scale_one).astype(LOW)
        projected = dot(normed, qkv_full, NN)
        query_raw = projected[:, : H * HD].reshape(length, H, HD)
        keys_raw = projected[:, H * HD : (H + KV) * HD].reshape(length, KV, HD)
        values = projected[:, (H + KV) * HD :].reshape(length, KV, HD).astype(LOW)
        cosine, sine = rotary_tables(places_of[seq][1])
        cosine, sine = cosine[:, None, :], sine[:, None, :]
        query_scale, keys_scale = rms_scale(query_raw), rms_scale(keys_raw)
        query_rot = rotary(query_raw * query_scale * head_gains[0], cosine, sine).astype(LOW)
        keys_rot = rotary(keys_raw * keys_scale * head_gains[1], cosine, sine).astype(LOW)
        kv = jnp.concatenate([keys_rot, values], axis=-1).transpose(1, 0, 2)
        kv_all = lax.all_gather(kv, "ctx", axis=0)
        query = query_rot * LOW(1.0 / math.sqrt(HD))
        query = query.reshape(length, KV, G, HD).transpose(1, 2, 0, 3)
        query = jnp.pad(query, ((0, 0),) * 3 + ((0, HD),)).reshape(KV, G * length, 2 * HD)
        index = rank_of[seq] * length + jnp.arange(length, dtype=jnp.int32)
        start = jnp.where(places_of[seq][0] == 0, 0, index - places_of[seq][1])
        full = jnp.minimum((jnp.max(start) + length - 1) // length, rank_of[seq])
        low = jnp.minimum(jnp.min(start) // length, full)
        meta = jnp.stack([rank_of[seq], low, full]).astype(jnp.int32)
        start = jnp.tile(start[None, :], (1, G))
        index = jnp.tile(index[None, :], (1, G))
        keep = (inputs, scale_one, normed, query_raw, keys_raw, query_scale, keys_scale)
        return keep + (cosine, sine), (meta, start, index, query, kv_all)

    def feed(seq, keep, attended):
        middle = keep[0] + dot(attended, out_full, NN)
        scale_two = rms_scale(middle)
        feed_in = (middle * scale_two).astype(LOW)
        feed_in = feed_in.reshape(length, n_dp, n_ctx, own).transpose(0, 2, 1, 3)
        feed_all = jnp.concatenate(gather_dp(feed_in.reshape(length, width)), axis=0)
        return middle, scale_two, feed_all

    def hidden_units(seq, feed_all, grad_all):
        gate = dot(feed_all, gate_up_part[:, :part], NN)
        up = dot(feed_all, gate_up_part[:, part:], NN)
        sigmoid_gate = jax.nn.sigmoid(gate)
        silu_gate = gate * sigmoid_gate
        hidden = (silu_gate * up).astype(LOW)
        d_hidden = dot(grad_all, down_part, NT)
        d_gate = d_hidden * up * sigmoid_gate * (1.0 + gate * (1.0 - sigmoid_gate))
        d_up = d_hidden * silu_gate
        d_gate_up = jnp.concatenate([d_gate.astype(LOW), d_up.astype(LOW)], axis=1)
        d_feed = reduce_dp(jnp.split(dot(d_gate_up, gate_up_part, NT).astype(LOW), n_dp))
        result = reduce_dp(jnp.split(dot(hidden, down_part, NN).astype(LOW), n_dp))
        d_feed = d_feed.reshape(length, n_ctx, n_dp, own).transpose(0, 2, 1, 3)
        return hidden, d_gate_up, d_feed.reshape(length, width), result

    def attention_grad(seq, middle, scale_two, d_feed, attended):
        d_middle = grads_of[seq].astype(F32) + norm_back(d_feed, middle, scale_two)
        d_middle_low = d_middle.astype(LOW)
        d_attended = dot(d_middle_low, out_full, NT).astype(LOW)
        inner = (
            jnp.sum(
                (d_attended.astype(F32) * attended.astype(F32)).reshape(length, KV, G, HD), axis=-1
            )
            .transpose(1, 2, 0)
            .reshape(KV, 1, G * length)
        )
        grad_items = d_attended.reshape(length, KV, G, HD).transpose(1, 2, 0, 3)
        grad_items = jnp.pad(grad_items, ((0, 0),) * 3 + ((HD, 0),))
        return d_middle, d_middle_low, grad_items.reshape(KV, G * length, 2 * HD), inner

    def project_back(seq, keep, d_query_rot, d_kv):
        inputs, scale_one, normed, query_raw, keys_raw, query_scale, keys_scale, cosine, sine = keep
        d_kv = lax.psum_scatter(d_kv, "ctx", scatter_dimension=0, tiled=False)
        d_kv = d_kv.transpose(1, 0, 2).astype(F32)
        d_query_norm = rotary_back(d_query_rot.reshape(length, H, HD), cosine, sine)
        d_query = norm_back(d_query_norm * head_gains[0], query_raw, query_scale)
        d_keys_norm = rotary_back(d_kv[..., :HD], cosine, sine)
        d_keys = norm_back(d_keys_norm * head_gains[1], keys_raw, keys_scale)
        d_projected = jnp.concatenate(
            [
                d_query.astype(LOW).reshape(length, H * HD),
                d_keys.astype(LOW).reshape(length, KV * HD),
                d_kv[..., HD:].astype(LOW).reshape(length, KV * HD),
            ],
            axis=1,
        )
        head_terms = jnp.stack(
            [
                jnp.sum(d_query_norm * query_raw * query_scale, axis=(0, 1)),
                jnp.sum(d_keys_norm * keys_raw * keys_scale, axis=(0, 1)),
            ]
        )
        d_inputs = norm_back(dot(d_projected, qkv_full, NT), inputs, scale_one)
        return d_projected, head_terms, d_inputs

    each = range(seqs)
    grad_alls = [jnp.concatenate(gather_dp(grads_of[seq]), axis=0) for seq in each]
    keeps, items = zip(*[project(seq) for seq in each])
    attendeds, logs = zip(*[attend(seq % 2 == 1, *items[seq]) for seq in each])
    middles, scales, feed_alls = zip(*[feed(seq, keeps[seq], attendeds[seq]) for seq in each])
    hiddens, d_gate_ups, d_feeds, results = zip(
        *[hidden_units(seq, feed_alls[seq], grad_alls[seq]) for seq in each]
    )
    outputs = [(middles[seq] + results[seq]).astype(LOW) for seq in each]
    gate_up_sum = sum(dot(feed_alls[seq], d_gate_ups[seq], TN) for seq in each).astype(LOW)
    gate_up_grad = lax.psum_scatter(gate_up_sum, "ctx", scatter_dimension=0, tiled=True)
    gate_up_grad = exchange(gate_up_grad.reshape(n_dp, own, 2 * part), "dp")
    gate_up_grad = (
        gate_up_grad.reshape(n_dp, own, 2, part).transpose(1, 2, 0, 3).reshape(own, 2 * ff)
    ).astype(F32)
    down_sum = sum(dot(hiddens[seq], grad_alls[seq], TN) for seq in each).astype(LOW)
    down_grad = lax.psum_scatter(down_sum, "ctx", scatter_dimension=0, tiled=True).astype(F32)

    d_middles, d_middle_lows, grad_items, inners = zip(
        *[attention_grad(s, middles[s], scales[s], d_feeds[s], attendeds[s]) for s in each]
    )
    d_queries, d_kvs = zip(
        *[attend_back(s % 2 == 1, *items[s], grad_items[s], logs[s], inners[s]) for s in each]
    )
    d_projecteds, head_terms, d_inputs = zip(
        *[project_back(s, keeps[s], d_queries[s], d_kvs[s]) for s in each]
    )
    head_grad = lax.psum(sum(head_terms), everyone)
    input_grads = [(d_middles[s] + d_inputs[s]).astype(LOW) for s in each]
    attention_sum = jnp.concatenate(
        [
            sum(dot(keeps[s][2], d_projecteds[s], TN) for s in each).astype(LOW),
            sum(dot(attendeds[s], d_middle_lows[s], TN) for s in each).astype(LOW),
        ],
        axis=1,
    )
    attention_weight_grad = lax.psum_scatter(
        attention_sum, everyone, scatter_dimension=0, tiled=True
    ).astype(F32)
    qkv_grad = attention_weight_grad[:, : qkv_weight.shape[1]]
    out_grad = attention_weight_grad[:, qkv_weight.shape[1] :]

    def placed(values):
        return jnp.stack([mirror(values[s]) if s % 2 == 1 else values[s] for s in each])

    norm_grad = jnp.stack(
        [jnp.sum(qkv_low * qkv_grad, axis=1), jnp.sum(gate_up_low * gate_up_grad, axis=1)]
    )
    qkv_new = adam(qkv_weight, qkv_first, qkv_second, qkv_grad * gain_one, RATE_QKV, DECAY)
    out_new = adam(out_weight, out_first, out_second, out_grad, RATE_OUT, DECAY)
    gate_up_new = adam(
        gate_up_weight,
        gate_up_first,
        gate_up_second,
        gate_up_grad * gain_two,
        RATE_GATE_UP,
        DECAY,
    )
    down_new = adam(down_weight, down_first, down_second, down_grad, RATE_DOWN, DECAY)
    norm_new = adam(norm_gains, norm_first, norm_second, norm_grad, RATE_GAIN, 0.0)
    head_new = adam(head_gains, head_first, head_second, head_grad, RATE_GAIN, 0.0)
    return (
        placed(outputs),
        placed(input_grads),
        *qkv_new,
        *out_new,
        *gate_up_new,
        *down_new,
        *norm_new,
        *head_new,
    )


def solution(mesh):
    tokens_spec = P("dp", "ctx", None)
    matrix = P(("dp", "ctx"), None)
    gains = P(None, ("dp", "ctx"))
    in_specs = (
        (tokens_spec,) * 2 + (P("dp", "ctx"),) * 2 + (matrix,) * 12 + (gains,) * 3 + (P(),) * 3
    )
    out_specs = (tokens_spec,) * 2 + (matrix,) * 12 + (gains,) * 3 + (P(),) * 3
    return jax.shard_map(body, mesh=mesh, in_specs=in_specs, out_specs=out_specs, check_vma=False)
```

```python
import functools
import math

import jax
import jax.numpy as jnp
from jax import lax
from jax.experimental import pallas as pl
from jax.experimental.pallas import tpu as pltpu
from jax.sharding import PartitionSpec as P

H = 32
KV = 8
HD = 64
G = H // KV
STEP = 5

EPS = 1e-05
ROPE_BASE = 1000000.0
BETA_ONE = 0.9
BETA_TWO = 0.95
ADAM_EPS = 1e-08
DECAY = 0.1
RATE_QKV = 0.05
RATE_OUT = 0.3
RATE_GATE_UP = 0.05
RATE_DOWN = 0.03
RATE_GAIN = 0.5

LOW = jnp.bfloat16
F32 = jnp.float32


def rms_scale(values):
    return lax.rsqrt(jnp.mean(values * values, axis=-1, keepdims=True) + EPS)


def norm_back(scaled, values, inv_rms):
    inner = jnp.mean(scaled * values, axis=-1, keepdims=True)
    return inv_rms * (scaled - values * inv_rms * inv_rms * inner)


def rotary(values, cosine, sine):
    first, second = values[..., : HD // 2], values[..., HD // 2 :]
    return jnp.concatenate([first * cosine - second * sine, second * cosine + first * sine], axis=-1)


def rotary_back(grad, cosine, sine):
    first, second = grad[..., : HD // 2], grad[..., HD // 2 :]
    return jnp.concatenate([first * cosine + second * sine, second * cosine - first * sine], axis=-1)


def rotary_tables(place_ids):
    freqs = ROPE_BASE ** (-(jnp.arange(HD // 2).astype(F32) * 2.0 / HD))
    angles = place_ids.astype(F32)[..., None] * freqs
    return (jnp.cos(angles), jnp.sin(angles))


def dot(left, right, dims):
    return lax.dot_general(left, right, (dims, ((), ())), preferred_element_type=F32)


NN = ((1,), (0,))
NT = ((1,), (1,))
TN = ((0,), (0,))


def adam(master, moment_one, moment_two, grad, step_rate, decay_rate):
    first_new = BETA_ONE * moment_one + (1.0 - BETA_ONE) * grad
    second_new = BETA_TWO * moment_two + (1.0 - BETA_TWO) * grad * grad
    first_hat = first_new / (1.0 - BETA_ONE**STEP)
    second_hat = second_new / (1.0 - BETA_TWO**STEP)
    master_new = master - step_rate * (
        first_hat / (jnp.sqrt(second_hat) + ADAM_EPS) + decay_rate * master
    )
    return (master_new, first_new, second_new)


def chunk_mask(chunk, length, start, query_index):
    key_index = chunk * length + lax.broadcasted_iota(jnp.int32, (length, start.shape[1]), 0)
    return (key_index >= start) & (key_index <= query_index)


def for_chunks(meta_ref, step):
    block = pl.program_id(0)
    place, low, full = meta_ref[block, 0], meta_ref[block, 1], meta_ref[block, 2]

    @pl.loop(low, full)
    def _(chunk):
        step(chunk, True)

    @pl.loop(full, place)
    def _(chunk):
        step(chunk, False)

    step(place, True)


def attend_kernel(meta_ref, start_ref, index_ref, query_ref, kv_ref, out_ref, log_ref, acc_ref):
    length = query_ref.shape[2] // G
    start, query_index = start_ref[0], index_ref[0]
    turned = meta_ref[pl.program_id(0), 3]
    lane = lax.broadcasted_iota(jnp.int32, (length, 2 * HD), 1)
    acc_ref[...] = jnp.zeros_like(acc_ref)

    def step(chunk, masked):
        slot = chunk + turned * (kv_ref.shape[0] - 1 - 2 * chunk)
        kv = kv_ref[slot, 0, 0]
        ones_v = jnp.where(lane < HD, jnp.ones_like(kv), kv)
        probs = jnp.exp(dot(kv, query_ref[0, 0], NT))
        if masked:
            probs = jnp.where(chunk_mask(chunk, length, start, query_index), probs, 0.0)
        acc_ref[...] += dot(ones_v, probs.astype(LOW), TN)

    for_chunks(meta_ref, step)
    total = acc_ref[:1, :]
    log_ref[0, 0] = jnp.log(total)
    mixed = acc_ref[HD:, :] / total
    rows = [mixed[:, head * length : (head + 1) * length] for head in range(G)]
    out_ref[0] = jnp.concatenate(rows, axis=0).T.astype(out_ref.dtype)


def attend_back_kernel(
    meta_ref,
    start_ref,
    index_ref,
    query_ref,
    kv_ref,
    grad_ref,
    log_ref,
    inner_ref,
    _,
    dq_ref,
    dkv_ref,
    acc_ref,
):
    length = query_ref.shape[2] // G
    start, query_index = start_ref[0], index_ref[0]
    turned = meta_ref[pl.program_id(0), 3]
    acc_ref[...] = jnp.zeros_like(acc_ref)
    dkv_ref[...] = jnp.zeros_like(dkv_ref)

    def step(chunk, masked):
        slot = chunk + turned * (kv_ref.shape[0] - 1 - 2 * chunk)
        kv = kv_ref[slot, 0, 0]
        total = jnp.zeros((length, 2 * HD), F32)
        for head in range(G):
            part = pl.ds(head * length, length)
            query, grad = query_ref[0, 0, part], grad_ref[0, 0, part]
            probs = jnp.exp(dot(kv, query, NT) - log_ref[0, 0, :, part])
            if masked:
                mask = chunk_mask(chunk, length, start[:, :length], query_index[:, :length])
                probs = jnp.where(mask, probs, 0.0)
            d_probs = dot(kv, grad, NT)
            d_scores = (probs * (d_probs - inner_ref[0, 0, :, part])).astype(LOW)
            total = total + dot(d_scores, query, NN) + dot(probs.astype(LOW), grad, NN)
            acc_ref[:, part] += dot(kv, d_scores, TN)
        dkv_ref[slot, 0, 0] = total.astype(dkv_ref.dtype)

    for_chunks(meta_ref, step)
    rows = [acc_ref[:HD, head * length : (head + 1) * length] for head in range(G)]
    dq_ref[0] = jnp.concatenate(rows, axis=0).T * (1.0 / math.sqrt(HD))


def attention_specs(n_ctx, length):
    query = pl.BlockSpec((1, 1, G * length, 2 * HD), lambda b, h, *_: (b, h, 0, 0))
    kv = pl.BlockSpec((n_ctx, 1, 1, length, 2 * HD), lambda b, h, *_: (0, b, h, 0, 0))
    row = pl.BlockSpec((1, 1, 1, G * length), lambda b, h, *_: (b, h, 0, 0))
    start = pl.BlockSpec((1, 1, G * length), lambda b, h, *_: (b, 0, 0))
    natural = pl.BlockSpec((1, length, G * HD), lambda b, h, *_: (b, 0, h))
    return query, kv, row, start, natural


def attend(meta, start, index, query, kv_all):
    n_ctx, blocks, heads, length, _ = kv_all.shape
    q_spec, kv_spec, row_spec, start_spec, natural = attention_specs(n_ctx, length)
    pairs = blocks * heads * G * length * n_ctx * length
    return pl.pallas_call(
        attend_kernel,
        grid_spec=pltpu.PrefetchScalarGridSpec(
            num_scalar_prefetch=1,
            grid=(blocks, heads),
            in_specs=[start_spec, start_spec, q_spec, kv_spec],
            out_specs=[natural, row_spec],
            scratch_shapes=[pltpu.VMEM((2 * HD, G * length), F32)],
        ),
        out_shape=[
            jax.ShapeDtypeStruct((blocks, length, heads * G * HD), LOW),
            jax.ShapeDtypeStruct((blocks, heads, 1, G * length), F32),
        ],
        compiler_params=pltpu.CompilerParams(vmem_limit_bytes=40 * 2**20),
        cost_estimate=pl.CostEstimate(
            flops=pairs * 32, bytes_accessed=2**20, transcendentals=0
        ),
        name="attend",
    )(meta, start, index, query, kv_all)


def attend_back(meta, start, index, query, kv_all, grad, log_total, inner, other):
    n_ctx, blocks, heads, length, _ = kv_all.shape
    q_spec, kv_spec, row_spec, start_spec, natural = attention_specs(n_ctx, length)
    pairs = blocks * heads * G * length * n_ctx * length
    return pl.pallas_call(
        attend_back_kernel,
        grid_spec=pltpu.PrefetchScalarGridSpec(
            num_scalar_prefetch=1,
            grid=(blocks, heads),
            in_specs=[start_spec, start_spec, q_spec, kv_spec, q_spec, row_spec, row_spec]
            + [pl.BlockSpec(memory_space=pl.ANY)],
            out_specs=[natural, kv_spec],
            scratch_shapes=[pltpu.VMEM((2 * HD, G * length), F32)],
        ),
        out_shape=[
            jax.ShapeDtypeStruct((blocks, length, heads * G * HD), F32),
            jax.ShapeDtypeStruct(kv_all.shape, LOW),
        ],
        compiler_params=pltpu.CompilerParams(vmem_limit_bytes=40 * 2**20),
        cost_estimate=pl.CostEstimate(
            flops=pairs * 64, bytes_accessed=2**20, transcendentals=0
        ),
        name="attend_back",
    )(meta, start, index, query, kv_all, grad, log_total, inner, other)


MESH = pl.DeviceIdType.MESH
DMA = pltpu.SemaphoreType.DMA


def flip(rank, shift):
    result, bit = rank, 1
    while bit <= shift:
        if shift & bit:
            result = result + bit - 2 * bit * ((rank // bit) % 2)
        bit *= 2
    return result


class Place:
    def __init__(self, n_dp, n_ctx):
        self.n_dp, self.n_ctx = n_dp, n_ctx
        self.last = n_ctx // 2 - 1
        self.dp, self.ctx = lax.axis_index("dp"), lax.axis_index("ctx")
        self.column, self.core = self.ctx // 2, self.ctx % 2
        self.sibling = (self.dp, self.ctx + 1 - 2 * self.core)
        self.above = (self.dp, self.ctx + 2)
        self.below = (self.dp, self.ctx - 2)
        self.opposite = (self.dp, n_ctx - 1 - self.ctx)

    def peer(self, shift):
        return (flip(self.dp, shift), self.ctx)

    def meet(self, along_dp, along_ctx, across):
        barrier = pltpu.get_barrier_semaphore()

        def greet(device):
            pl.semaphore_signal(barrier, inc=1, device_id=device, device_id_type=MESH)

        count = 0
        if across:
            greet(self.opposite)
            count = 1
        if along_dp:
            for shift in range(1, self.n_dp):
                greet(self.peer(shift))
            count = count + self.n_dp - 1
        if along_ctx:
            greet(self.sibling)
            count = count + 1
            if self.last > 0:
                pl.when(self.column > 0)(lambda: greet(self.below))
                pl.when(self.column < self.last)(lambda: greet(self.above))
                count = count + (self.column + self.last - 1) // self.last
                count = count + (2 * self.last - 1 - self.column) // self.last
        pl.semaphore_wait(barrier, count)


def remote(source, target, send_sem, recv_sem, device):
    return pltpu.make_async_remote_copy(
        src_ref=source,
        dst_ref=target,
        send_sem=send_sem,
        recv_sem=recv_sem,
        device_id=device,
        device_id_type=MESH,
    )


CHUNKS = 2


class GatherDp:
    along_dp, along_ctx, across = True, False, False

    def __init__(self, values, n_dp, n_ctx):
        self.rows = values.shape[0]
        self.operand_spec = pl.BlockSpec(memory_space=pl.ANY)
        self.out_spec = pl.BlockSpec(memory_space=pl.ANY)
        self.out_shape = jax.ShapeDtypeStruct((n_dp, *values.shape), values.dtype)
        self.scratch = [DMA(()), DMA((n_dp, CHUNKS, 2)), DMA((n_dp, CHUNKS, 2))]

    def phases(self, at, own, out, local, send, recv):
        size = self.rows // CHUNKS
        halves = at.n_dp == 4
        direct = (1, 2) if halves else tuple(range(1, at.n_dp))
        mine = pltpu.make_async_copy(own, out.at[0], local)

        def straight(shift, chunk):
            part = pl.ds(chunk * size, size)
            return remote(
                own.at[part],
                out.at[shift, part],
                send.at[shift, chunk, 0],
                recv.at[shift, chunk, 0],
                at.peer(shift),
            )

        def turned(shift, chunk):
            part = pl.ds(chunk * size + (2 - shift) * (size // 2), size // 2)
            return remote(
                out.at[3 - shift, part],
                out.at[3, part],
                send.at[3, chunk, shift - 1],
                recv.at[3, chunk, shift - 1],
                at.peer(shift),
            )

        def begin():
            for chunk in range(CHUNKS):
                for shift in direct:
                    straight(shift, chunk).start()
            mine.start()

        def middle():
            for chunk in range(CHUNKS):
                for shift in direct:
                    straight(shift, chunk).wait_recv()
                    if halves:
                        turned(3 - shift, chunk).start()

        def end():
            for chunk in range(CHUNKS):
                if halves:
                    for shift in direct:
                        turned(shift, chunk).wait()
                for shift in direct:
                    straight(shift, chunk).wait_send()
            mine.wait()

        return [begin, middle, end]


class SumDp:
    along_dp, along_ctx, across = True, False, False

    def __init__(self, values, n_dp, n_ctx):
        _, self.rows, width = values.shape
        size = self.rows // CHUNKS
        self.operand_spec = pl.BlockSpec(memory_space=pltpu.VMEM)
        self.out_spec = pl.BlockSpec(memory_space=pltpu.VMEM)
        self.out_shape = jax.ShapeDtypeStruct((self.rows, width), F32)
        peers = 2 if n_dp == 4 else n_dp - 1
        self.scratch = [
            pltpu.VMEM((2, CHUNKS, size // 2, width), LOW),
            pltpu.VMEM((2, CHUNKS, size // 2, width), LOW),
            pltpu.VMEM((peers, CHUNKS, 2, size // 2, width), LOW),
            DMA((2, CHUNKS)),
            DMA((2, CHUNKS)),
            DMA((peers, CHUNKS, 2)),
            DMA((peers, CHUNKS, 2)),
        ]

    def phases(self, at, parts, out, arrived, joined, sums, t_send, t_recv, p_send, p_recv):
        size = self.rows // CHUNKS
        half = size // 2
        halves = at.n_dp == 4
        direct = (1, 2) if halves else tuple(range(1, at.n_dp))

        def rows(chunk, which):
            return pl.ds(chunk * size + which * half, half)

        def turning(shift, chunk):
            return remote(
                parts.at[3, rows(chunk, shift - 1)],
                arrived.at[shift - 1, chunk],
                t_send.at[shift - 1, chunk],
                t_recv.at[shift - 1, chunk],
                at.peer(shift),
            )

        def final(shift, chunk, which):
            source = parts.at[shift, rows(chunk, which)]
            if halves and which == 2 - shift:
                source = joined.at[shift - 1, chunk]
            return remote(
                source,
                sums.at[shift - 1, chunk, which],
                p_send.at[shift - 1, chunk, which],
                p_recv.at[shift - 1, chunk, which],
                at.peer(shift),
            )

        def begin():
            for chunk in range(CHUNKS):
                if halves:
                    for shift in direct:
                        turning(shift, chunk).start()
                for shift in direct:
                    for which in (0, 1):
                        if not halves or which != 2 - shift:
                            final(shift, chunk, which).start()

        def middle():
            if halves:
                for chunk in range(CHUNKS):
                    for shift in direct:
                        turning(shift, chunk).wait_recv()
                        to = 3 - shift
                        mine = parts[to, rows(chunk, shift - 1)].astype(F32)
                        came = arrived[shift - 1, chunk].astype(F32)
                        joined[to - 1, chunk] = (mine + came).astype(LOW)
                        final(to, chunk, shift - 1).start()

        def end():
            for chunk in range(CHUNKS):
                for which in (0, 1):
                    total = parts[0, rows(chunk, which)].astype(F32)
                    for shift in direct:
                        final(shift, chunk, which).wait_recv()
                        total = total + sums[shift - 1, chunk, which].astype(F32)
                    out[rows(chunk, which)] = total
            for chunk in range(CHUNKS):
                for shift in direct:
                    if halves:
                        turning(shift, chunk).wait_send()
                    for which in (0, 1):
                        final(shift, chunk, which).wait_send()

        return [begin, middle, end]


class GatherCtx:
    along_dp, along_ctx, across = False, True, False

    def __init__(self, values, n_dp, n_ctx):
        columns = n_ctx // 2
        self.operand_spec = pl.BlockSpec(memory_space=pl.ANY)
        self.out_spec = pl.BlockSpec(memory_space=pl.ANY)
        self.out_shape = jax.ShapeDtypeStruct((n_ctx, *values.shape), values.dtype)
        self.scratch = [DMA(())] + [DMA((columns,))] * 5

    def phases(self, at, own, out, local, up_send, down_send, recv, sib_send, sib_recv):
        mine = pltpu.make_async_copy(own, out.at[at.ctx], local)

        def travel(column, sem, device):
            ref = out.at[2 * column + at.core]
            source = ref
            return remote(source, ref, sem.at[column], recv.at[column], device)

        def to_sibling(column):
            ref = out.at[2 * column + at.core]
            return remote(ref, ref, sib_send.at[column], sib_recv.at[column], at.sibling)

        def from_sibling(column):
            ref = out.at[2 * column + 1 - at.core]
            remote(ref, ref, sib_send.at[column], sib_recv.at[column], at.sibling).wait_recv()

        def pass_on(column):
            pl.when((column <= at.column) & (at.column < at.last))(
                lambda: travel(column, up_send, at.above).start()
            )
            pl.when((column >= at.column) & (at.column > 0))(
                lambda: travel(column, down_send, at.below).start()
            )
            to_sibling(column).start()

        def begin():
            mine.start()
            mine.wait()
            pass_on(at.column)

        def middle():
            @pl.loop(1, 2 * at.last + 1)
            def _(count):
                away = (count + 1) // 2
                column = at.column + away - 2 * away * (count % 2)

                @pl.when((column >= 0) & (column <= at.last))
                def _():
                    travel(column, up_send, at.sibling).wait_recv()
                    pass_on(column)

        def end():
            @pl.loop(0, at.last + 1)
            def _(column):
                from_sibling(column)
                to_sibling(column).wait_send()
                pl.when((column <= at.column) & (at.column < at.last))(
                    lambda: travel(column, up_send, at.above).wait_send()
                )
                pl.when((column >= at.column) & (at.column > 0))(
                    lambda: travel(column, down_send, at.below).wait_send()
                )

        return [begin, middle, end]


class SumCtx:
    along_dp, along_ctx, across = False, True, False

    def __init__(self, values, n_dp, n_ctx):
        columns = n_ctx // 2
        _, rows, width = values.shape
        self.operand_spec = pl.BlockSpec(memory_space=pltpu.VMEM)
        self.out_spec = pl.BlockSpec(memory_space=pltpu.VMEM)
        self.out_shape = jax.ShapeDtypeStruct((rows, width), F32)
        block = pltpu.VMEM((columns, rows, width), LOW)
        self.scratch = [block] * 4 + [DMA((columns,))] * 6

    def phases(
        self,
        at,
        parts,
        out,
        acc,
        from_sib,
        from_below,
        from_above,
        sib_send,
        sib_recv,
        up_send,
        up_recv,
        down_send,
        down_recv,
    ):
        def to_sibling(column):
            return remote(
                parts.at[2 * column + 1 - at.core],
                from_sib.at[column],
                sib_send.at[column],
                sib_recv.at[column],
                at.sibling,
            )

        def to_above(column):
            return remote(
                acc.at[column],
                from_below.at[column],
                up_send.at[column],
                up_recv.at[column],
                at.above,
            )

        def to_below(column):
            return remote(
                acc.at[column],
                from_above.at[column],
                down_send.at[column],
                down_recv.at[column],
                at.below,
            )

        def farthest_first(step):
            @pl.loop(0, at.last + 1)
            def _(count):
                odd = count % 2
                step((1 - odd) * (at.last - count // 2) + odd * (count // 2))

        def begin():
            farthest_first(lambda column: to_sibling(column).start())

        def line(column):
            to_sibling(column).wait_recv()
            mine = parts[2 * column + at.core].astype(F32) + from_sib[column].astype(F32)
            acc[column] = mine.astype(LOW)

            def add(came):
                acc[column] = (acc[column].astype(F32) + came[column].astype(F32)).astype(LOW)

            @pl.when(column > at.column)
            def _():
                @pl.when(at.column > 0)
                def _():
                    to_above(column).wait_recv()
                    add(from_below)

                to_above(column).start()

            @pl.when(column < at.column)
            def _():
                @pl.when(at.column < at.last)
                def _():
                    to_below(column).wait_recv()
                    add(from_above)

                to_below(column).start()

        def middle():
            farthest_first(line)

        def end():
            out[...] = acc[at.column].astype(F32)

            @pl.when(at.column > 0)
            def _():
                to_above(at.column).wait_recv()
                out[...] += from_below[at.column].astype(F32)

            @pl.when(at.column < at.last)
            def _():
                to_below(at.column).wait_recv()
                out[...] += from_above[at.column].astype(F32)

            @pl.loop(0, at.last + 1)
            def _(column):
                to_sibling(column).wait_send()
                pl.when(column > at.column)(lambda: to_above(column).wait_send())
                pl.when(column < at.column)(lambda: to_below(column).wait_send())

        return [begin, middle, end]


class Mirror:
    along_dp, along_ctx, across = False, False, True

    def __init__(self, values, n_dp, n_ctx):
        self.operand_spec = pl.BlockSpec(memory_space=pl.ANY)
        self.out_spec = pl.BlockSpec(memory_space=pl.ANY)
        self.out_shape = jax.ShapeDtypeStruct(values.shape, values.dtype)
        self.scratch = [DMA(()), DMA(())]

    def phases(self, at, own, out, send, recv):
        copy = remote(own, out, send, recv, at.opposite)
        return [copy.start, lambda: None, copy.wait]


class ExchangeDp:
    along_dp, along_ctx, across = True, False, False

    def __init__(self, values, n_dp, n_ctx):
        self.operand_spec = pl.BlockSpec(memory_space=pl.ANY)
        self.out_spec = pl.BlockSpec(memory_space=pl.ANY)
        self.out_shape = jax.ShapeDtypeStruct(values.shape, values.dtype)
        self.scratch = [DMA(()), DMA((n_dp,)), DMA((n_dp,))]

    def phases(self, at, blocks, out, local, send, recv):
        mine = pltpu.make_async_copy(blocks.at[at.dp], out.at[at.dp], local)

        def to_peer(shift):
            return remote(
                blocks.at[flip(at.dp, shift)],
                out.at[at.dp],
                send.at[shift],
                recv.at[shift],
                at.peer(shift),
            )

        def from_peer(shift):
            ref = out.at[flip(at.dp, shift)]
            return remote(ref, ref, send.at[shift], recv.at[shift], at.peer(shift))

        def begin():
            for shift in range(1, at.n_dp):
                to_peer(shift).start()
            mine.start()

        def end():
            for shift in range(1, at.n_dp):
                from_peer(shift).wait_recv()
                to_peer(shift).wait_send()
            mine.wait()

        return [begin, lambda: None, end]


def move_kernel(jobs, n_dp, n_ctx, n_others, *refs):
    at = Place(n_dp, n_ctx)
    operands, refs = refs[: len(jobs)], refs[len(jobs) + n_others :]
    outs, refs = refs[: len(jobs)], list(refs[len(jobs) :])
    lists = []
    for job, operand, out in zip(jobs, operands, outs):
        scratch = [refs.pop(0) for _ in job.scratch]
        lists.append(job.phases(at, operand, out, *scratch))
    at.meet(
        any(job.along_dp for job in jobs),
        any(job.along_ctx for job in jobs),
        any(job.across for job in jobs),
    )
    for phase in zip(*lists):
        for step in phase:
            step()


def move(collective_id, name, *kinds_and_values, others=()):
    n_dp, n_ctx = lax.axis_size("dp"), lax.axis_size("ctx")
    jobs = [kind(values, n_dp, n_ctx) for kind, values in kinds_and_values]
    values = [value for _, value in kinds_and_values]
    return pl.pallas_call(
        functools.partial(move_kernel, jobs, n_dp, n_ctx, len(others)),
        out_shape=[job.out_shape for job in jobs],
        in_specs=[job.operand_spec for job in jobs]
        + [pl.BlockSpec(memory_space=pl.ANY)] * len(others),
        out_specs=[job.out_spec for job in jobs],
        scratch_shapes=[piece for job in jobs for piece in job.scratch],
        compiler_params=pltpu.CompilerParams(
            collective_id=collective_id, has_side_effects=True, vmem_limit_bytes=58 * 2**20
        ),
        cost_estimate=pl.CostEstimate(flops=0, bytes_accessed=2**20, transcendentals=0),
        name=name,
    )(*values, *others)


def after(values, other):
    first = lax.slice(other.reshape(-1), (0,), (1,))[0]
    return jnp.where(first != first, jnp.zeros_like(values), values)


def pad_rows(values, rows):
    flat = values.reshape(-1)
    return jnp.pad(flat, (0, rows * 128 - flat.size)).reshape(rows, 128)


def pair_sum(blocks):
    while blocks.shape[0] > 1:
        blocks = blocks[0::2] + blocks[1::2]
    return blocks[0]


def body(
    tokens,
    output_grad,
    segment_ids,
    positions,
    qkv_weight,
    qkv_first,
    qkv_second,
    out_weight,
    out_first,
    out_second,
    gate_up_weight,
    gate_up_first,
    gate_up_second,
    down_weight,
    down_first,
    down_second,
    norm_gains,
    norm_first,
    norm_second,
    head_gains,
    head_first,
    head_second,
):
    n_dp, n_ctx = lax.axis_size("dp"), lax.axis_size("ctx")
    ctx_rank = lax.axis_index("ctx")
    seqs, length, width = tokens.shape
    own = norm_gains.shape[1]
    ff = down_weight.shape[0] * n_dp * n_ctx
    part = ff // n_dp

    kv_heads = KV // n_dp
    heads = kv_heads * G
    each = range(seqs)
    blocks = n_dp * seqs

    def spread_width(values):
        values = values.reshape(-1, n_dp, n_ctx, own).transpose(0, 2, 1, 3)
        return values.reshape(-1, width)

    def restore_width(values):
        values = values.reshape(-1, n_ctx, n_dp, own).transpose(0, 2, 1, 3)
        return values.reshape(-1, width)

    turned = jnp.arange(seqs, dtype=jnp.int32) % 2
    rank_of = ctx_rank + turned * (n_ctx - 1 - 2 * ctx_rank)
    places = jnp.stack([segment_ids, positions], axis=1)

    gain_one, gain_two = norm_gains[0][:, None], norm_gains[1][:, None]
    qkv_low = qkv_weight.astype(LOW).astype(F32)
    gate_up_low = gate_up_weight.astype(LOW).astype(F32)
    qkv_scaled = (qkv_low * gain_one).astype(LOW)
    qkv_blocks = jnp.concatenate(
        [
            block.reshape(own, n_dp, -1).transpose(1, 0, 2)
            for block in jnp.split(qkv_scaled, (H * HD, (H + KV) * HD), axis=1)
        ],
        axis=2,
    )
    qkv_cols = qkv_blocks.shape[2]

    def gather_ctx(values):
        return lax.all_gather(values.reshape(-1, values.shape[-1]), "ctx", axis=0, tiled=True)

    def scatter_ctx(values):
        return lax.psum_scatter(values, "ctx", scatter_dimension=0, tiled=True)

    qkv_mine, places_turned = move(
        1, "exchange_qkv", (ExchangeDp, qkv_blocks), (Mirror, pad_rows(places[1], 8))
    )
    qkv_part = gather_ctx(qkv_mine)
    down_part = gather_ctx(down_weight.astype(LOW))
    gate_up_blocks = (gate_up_low * gain_two).astype(LOW).reshape(own, 2, n_dp, part)
    gate_up_blocks = gate_up_blocks.transpose(2, 0, 1, 3).reshape(n_dp, own, 2 * part)
    places_turned = places_turned.reshape(-1)[: 2 * length].reshape(1, 2, length)
    places_of = jnp.concatenate([places[:1], places_turned], axis=0)

    def normed_rows(values):
        inputs = values.astype(F32)
        scale = rms_scale(inputs)
        return inputs, scale, spread_width((inputs * scale).astype(LOW))

    inputs_first, scale_first, normed = normed_rows(tokens[0])
    normed_first, tokens_turned, places_all = move(
        2,
        "gather_normed",
        (GatherDp, normed),
        (Mirror, tokens[1]),
        (GatherDp, pad_rows(places_of, 32)),
        others=(qkv_mine,),
    )
    inputs_second, scale_second, normed = normed_rows(tokens_turned)
    normed_second, grad_turned, gate_up_mine = move(
        3,
        "gather_normed",
        (GatherDp, normed),
        (Mirror, output_grad[1]),
        (ExchangeDp, gate_up_blocks),
    )
    inputs_of, scale_of = [inputs_first, inputs_second], [scale_first, scale_second]
    normed_of = [
        values.reshape(n_dp * length, width) for values in (normed_first, normed_second)
    ]
    projected_of = [
        dot(normed_of[s], qkv_part, NN).reshape(n_dp, length, qkv_cols) for s in each
    ]
    places_all = places_all.reshape(n_dp, -1)[:, : seqs * 2 * length].reshape(blocks, 2, length)

    projected = jnp.stack(projected_of, axis=1).reshape(blocks, length, qkv_cols)
    query_raw = projected[..., : heads * HD].reshape(blocks, length, heads, HD)
    keys_raw = projected[..., heads * HD : (heads + kv_heads) * HD]
    keys_raw = keys_raw.reshape(blocks, length, kv_heads, HD)
    values = projected[..., (heads + kv_heads) * HD :].astype(LOW)
    values = values.reshape(blocks, length, kv_heads, HD)
    segments, place_ids = places_all[:, 0], places_all[:, 1]
    cosine, sine = rotary_tables(place_ids)
    cosine, sine = cosine[:, :, None, :], sine[:, :, None, :]
    query_scale, keys_scale = rms_scale(query_raw), rms_scale(keys_raw)
    query_rot = rotary(query_raw * query_scale * head_gains[0], cosine, sine).astype(LOW)
    keys_rot = rotary(keys_raw * keys_scale * head_gains[1], cosine, sine).astype(LOW)
    kv = jnp.concatenate([keys_rot, values], axis=-1).transpose(0, 2, 1, 3)
    grads = jnp.concatenate([output_grad[0], grad_turned], axis=0)
    kv_all, grad_all = move(
        4,
        "gather_keys",
        (GatherCtx, kv.reshape(blocks * kv_heads * length, 2 * HD)),
        (GatherDp, grads),
        others=(down_part,),
    )
    out_part = gather_ctx(after(out_weight.astype(LOW), kv_all))
    gate_up_part = gather_ctx(after(gate_up_mine, kv_all))
    kv_all = kv_all.reshape(n_ctx, blocks, kv_heads, length, 2 * HD)
    grad_all = grad_all.reshape(blocks * length, width)
    query = query_rot * LOW(1.0 / math.sqrt(HD))
    query = query.reshape(blocks, length, kv_heads, G, HD).transpose(0, 2, 3, 1, 4)
    query = jnp.pad(query, ((0, 0),) * 4 + ((0, HD),))
    query = query.reshape(blocks, kv_heads, G * length, 2 * HD)
    place = jnp.tile(rank_of, n_dp)
    index = place[:, None] * length + jnp.arange(length, dtype=jnp.int32)
    start = jnp.where(segments == 0, 0, index - place_ids)
    full = jnp.minimum((jnp.max(start, axis=1) + length - 1) // length, place)
    low = jnp.minimum(jnp.min(start, axis=1) // length, full)
    meta = jnp.stack([place, low, full, jnp.tile(turned, n_dp)], axis=1)
    item = (
        meta,
        jnp.tile(start[:, None, :], (1, 1, G)),
        jnp.tile(index[:, None, :], (1, 1, G)),
        query,
        kv_all,
    )
    attended, log_total = attend(*item)
    attended = attended.reshape(blocks * length, heads * HD)

    def to_blocks(values):
        return values.astype(LOW).reshape(n_dp, -1, width)

    (mixed,) = move(5, "sum_mixed", (SumDp, to_blocks(dot(attended, out_part, NN))))
    inputs = jnp.concatenate(inputs_of, axis=0)
    middle = inputs + mixed
    scale_two = rms_scale(middle)
    (feed_all,) = move(
        6, "gather_feed", (GatherDp, spread_width((middle * scale_two).astype(LOW)))
    )
    feed_all = feed_all.reshape(blocks * length, width)

    gate = dot(feed_all, gate_up_part[:, :part], NN)
    up = dot(feed_all, gate_up_part[:, part:], NN)
    sigmoid_gate = jax.nn.sigmoid(gate)
    silu_gate = gate * sigmoid_gate
    hidden = (silu_gate * up).astype(LOW)
    d_hidden = dot(grad_all, down_part, NT)
    d_gate = d_hidden * up * sigmoid_gate * (1.0 + gate * (1.0 - sigmoid_gate))
    d_up = d_hidden * silu_gate
    d_gate_up = jnp.concatenate([d_gate.astype(LOW), d_up.astype(LOW)], axis=1)
    gate_up_sum = dot(feed_all, d_gate_up, TN).astype(LOW)
    down_sum = dot(hidden, grad_all, TN).astype(LOW)
    gate_up_grad = scatter_ctx(gate_up_sum)
    (d_feed,) = move(
        7,
        "sum_feed",
        (SumDp, to_blocks(dot(d_gate_up, gate_up_part, NT))),
        others=(gate_up_sum,),
    )
    d_middle = grads.astype(F32) + norm_back(restore_width(d_feed), middle, scale_two)
    d_middle_low = d_middle.astype(LOW)
    (d_middle_all,) = move(8, "gather_middle", (GatherDp, d_middle_low))
    down_scattered = scatter_ctx(after(after(down_sum, d_middle_all), gate_up_grad))
    d_middle_all = d_middle_all.reshape(blocks * length, width)

    d_attended = dot(d_middle_all, after(out_part, gate_up_grad), NT).astype(LOW)
    inner = (
        jnp.sum(
            (d_attended.astype(F32) * attended.astype(F32)).reshape(
                blocks, length, kv_heads, G, HD
            ),
            axis=-1,
        )
        .transpose(0, 2, 3, 1)
        .reshape(blocks, kv_heads, 1, G * length)
    )
    grad_items = d_attended.reshape(blocks, length, kv_heads, G, HD).transpose(0, 2, 3, 1, 4)
    grad_items = jnp.pad(grad_items, ((0, 0),) * 4 + ((HD, 0),))
    grad_items = grad_items.reshape(blocks, kv_heads, G * length, 2 * HD)
    d_query_rot, d_kv = attend_back(*item, grad_items, log_total, inner, gate_up_grad)
    out_sum = dot(attended, d_middle_all, TN).astype(LOW)
    out_grad = scatter_ctx(after(out_sum, down_scattered))
    d_kv, result, gate_up_grad = move(
        9,
        "sum_keys",
        (SumCtx, d_kv.reshape(n_ctx, blocks * kv_heads * length, 2 * HD)),
        (SumDp, to_blocks(dot(hidden, down_part, NN))),
        (ExchangeDp, gate_up_grad.reshape(n_dp, own, 2 * part)),
        others=(down_scattered,),
    )
    outputs = (middle + result).astype(LOW)
    d_kv = d_kv.reshape(blocks, kv_heads, length, 2 * HD).transpose(0, 2, 1, 3)
    d_query_rot = d_query_rot.reshape(blocks, length, heads, HD)
    d_query_norm = rotary_back(d_query_rot, cosine, sine)
    d_query = norm_back(d_query_norm * head_gains[0], query_raw, query_scale)
    d_keys_norm = rotary_back(d_kv[..., :HD], cosine, sine)
    d_keys = norm_back(d_keys_norm * head_gains[1], keys_raw, keys_scale)
    d_projected = jnp.concatenate(
        [
            d_query.astype(LOW).reshape(blocks, length, heads * HD),
            d_keys.astype(LOW).reshape(blocks, length, kv_heads * HD),
            d_kv[..., HD:].astype(LOW).reshape(blocks, length, kv_heads * HD),
        ],
        axis=2,
    ).reshape(n_dp, seqs, length, qkv_cols)
    head_terms = jnp.stack(
        [
            jnp.sum(d_query_norm * query_raw * query_scale, axis=(0, 1, 2)),
            jnp.sum(d_keys_norm * keys_raw * keys_scale, axis=(0, 1, 2)),
        ]
    )
    d_projected_of = [d_projected[:, s].reshape(n_dp * length, qkv_cols) for s in each]
    qkv_sum = sum(dot(normed_of[s], d_projected_of[s], TN) for s in each).astype(LOW)
    qkv_grad = scatter_ctx(qkv_sum)

    def input_gradient(seq, d_normed):
        d_inputs = norm_back(restore_width(d_normed), inputs_of[seq], scale_of[seq])
        return (d_middle[seq * length : (seq + 1) * length] + d_inputs).astype(LOW)

    d_normed, head_terms, outputs_second = move(
        10,
        "sum_normed",
        (SumDp, to_blocks(dot(d_projected_of[1], qkv_part, NT))),
        (GatherCtx, pad_rows(head_terms, 8)),
        (Mirror, outputs[length:]),
        others=(qkv_sum, out_grad),
    )
    head_terms = jnp.sum(head_terms, axis=0)
    d_normed, head_terms, input_grad_second, qkv_grad = move(
        11,
        "sum_normed",
        (SumDp, to_blocks(dot(d_projected_of[0], qkv_part, NT))),
        (GatherDp, pad_rows(head_terms, 32)),
        (Mirror, input_gradient(1, d_normed)),
        (ExchangeDp, qkv_grad.reshape(n_dp, own, qkv_cols)),
    )
    input_grad_first = input_gradient(0, d_normed)
    head_grad = pair_sum(head_terms)[:1].reshape(2, HD)
    qkv_grad = qkv_grad.astype(F32)
    qkv_grad = jnp.concatenate(
        [
            block.transpose(1, 0, 2).reshape(own, -1)
            for block in jnp.split(qkv_grad, (heads * HD, (heads + kv_heads) * HD), axis=2)
        ],
        axis=1,
    )
    out_grad = out_grad.astype(F32)
    down_grad = down_scattered.astype(F32)
    gate_up_grad = gate_up_grad.reshape(n_dp, own, 2, part).transpose(1, 2, 0, 3)
    gate_up_grad = gate_up_grad.reshape(own, 2 * ff).astype(F32)
    norm_grad = jnp.stack(
        [jnp.sum(qkv_low * qkv_grad, axis=1), jnp.sum(gate_up_low * gate_up_grad, axis=1)]
    )
    qkv_new = adam(qkv_weight, qkv_first, qkv_second, qkv_grad * gain_one, RATE_QKV, DECAY)
    out_new = adam(out_weight, out_first, out_second, out_grad, RATE_OUT, DECAY)
    gate_up_new = adam(
        gate_up_weight,
        gate_up_first,
        gate_up_second,
        gate_up_grad * gain_two,
        RATE_GATE_UP,
        DECAY,
    )
    down_new = adam(down_weight, down_first, down_second, down_grad, RATE_DOWN, DECAY)
    norm_new = adam(norm_gains, norm_first, norm_second, norm_grad, RATE_GAIN, 0.0)
    head_new = adam(head_gains, head_first, head_second, head_grad, RATE_GAIN, 0.0)
    return (
        jnp.stack([outputs[:length], outputs_second]),
        jnp.stack([input_grad_first, input_grad_second]),
        *qkv_new,
        *out_new,
        *gate_up_new,
        *down_new,
        *norm_new,
        *head_new,
    )


def solution(mesh):
    tokens_spec = P("dp", "ctx", None)
    matrix = P(("dp", "ctx"), None)
    gains = P(None, ("dp", "ctx"))
    in_specs = (
        (tokens_spec,) * 2 + (P("dp", "ctx"),) * 2 + (matrix,) * 12 + (gains,) * 3 + (P(),) * 3
    )
    out_specs = (tokens_spec,) * 2 + (matrix,) * 12 + (gains,) * 3 + (P(),) * 3
    return jax.shard_map(body, mesh=mesh, in_specs=in_specs, out_specs=out_specs, check_vma=False)
```

```python
import functools
import math

import jax
import jax.numpy as jnp
from jax import lax
from jax.experimental import pallas as pl
from jax.experimental.pallas import tpu as pltpu
from jax.sharding import PartitionSpec as P

H = 32
KV = 8
HD = 64
G = H // KV
STEP = 5

EPS = 1e-05
ROPE_BASE = 1000000.0
BETA_ONE = 0.9
BETA_TWO = 0.95
ADAM_EPS = 1e-08
DECAY = 0.1
RATE_QKV = 0.05
RATE_OUT = 0.3
RATE_GATE_UP = 0.05
RATE_DOWN = 0.03
RATE_GAIN = 0.5

LOW = jnp.bfloat16
F32 = jnp.float32


def rms_scale(values):
    return lax.rsqrt(jnp.mean(values * values, axis=-1, keepdims=True) + EPS)


def norm_back(scaled, values, inv_rms):
    inner = jnp.mean(scaled * values, axis=-1, keepdims=True)
    return inv_rms * (scaled - values * inv_rms * inv_rms * inner)


def rotary(values, cosine, sine):
    first, second = values[..., : HD // 2], values[..., HD // 2 :]
    return jnp.concatenate([first * cosine - second * sine, second * cosine + first * sine], axis=-1)


def rotary_back(grad, cosine, sine):
    first, second = grad[..., : HD // 2], grad[..., HD // 2 :]
    return jnp.concatenate([first * cosine + second * sine, second * cosine - first * sine], axis=-1)


def rotary_tables(place_ids):
    freqs = ROPE_BASE ** (-(jnp.arange(HD // 2).astype(F32) * 2.0 / HD))
    angles = place_ids.astype(F32)[..., None] * freqs
    return (jnp.cos(angles), jnp.sin(angles))


def dot(left, right, dims):
    return lax.dot_general(left, right, (dims, ((), ())), preferred_element_type=F32)


NN = ((1,), (0,))
NT = ((1,), (1,))
TN = ((0,), (0,))


def adam(master, moment_one, moment_two, grad, step_rate, decay_rate):
    first_new = BETA_ONE * moment_one + (1.0 - BETA_ONE) * grad
    second_new = BETA_TWO * moment_two + (1.0 - BETA_TWO) * grad * grad
    first_hat = first_new / (1.0 - BETA_ONE**STEP)
    second_hat = second_new / (1.0 - BETA_TWO**STEP)
    master_new = master - step_rate * (
        first_hat / (jnp.sqrt(second_hat) + ADAM_EPS) + decay_rate * master
    )
    return (master_new, first_new, second_new)


def chunk_mask(chunk, length, start, query_index):
    key_index = chunk * length + lax.broadcasted_iota(jnp.int32, (length, start.shape[1]), 0)
    return (key_index >= start) & (key_index <= query_index)


def for_chunks(meta_ref, step):
    block = pl.program_id(0)
    place, low, full = meta_ref[block, 0], meta_ref[block, 1], meta_ref[block, 2]

    @pl.loop(low, full)
    def _(chunk):
        step(chunk, True)

    @pl.loop(full, place)
    def _(chunk):
        step(chunk, False)

    step(place, True)


def pad_heads(rows_ref, values_ref, side):
    length = values_ref.shape[1]
    zeros = jnp.zeros((length, HD), rows_ref.dtype)
    for head in range(G):
        values = values_ref[0, :, head * HD : (head + 1) * HD]
        pair = [zeros, values] if side else [values, zeros]
        rows_ref[pl.ds(head * length, length), :] = jnp.concatenate(pair, axis=1)


def attend_kernel(meta_ref, start_ref, index_ref, query_ref, kv_ref, out_ref, log_ref, acc_ref, rows_ref):
    length = query_ref.shape[1]
    start, query_index = start_ref[0], index_ref[0]
    turned = meta_ref[pl.program_id(0), 3]
    lane = lax.broadcasted_iota(jnp.int32, (length, 2 * HD), 1)
    acc_ref[...] = jnp.zeros_like(acc_ref)
    pad_heads(rows_ref, query_ref, 0)

    def step(chunk, masked):
        slot = chunk + turned * (kv_ref.shape[0] - 1 - 2 * chunk)
        kv = kv_ref[slot, 0, 0]
        ones_v = jnp.where(lane < HD, jnp.ones_like(kv), kv)
        probs = jnp.exp(dot(kv, rows_ref[...], NT))
        if masked:
            probs = jnp.where(chunk_mask(chunk, length, start, query_index), probs, 0.0)
        acc_ref[...] += dot(ones_v, probs.astype(LOW), TN)

    for_chunks(meta_ref, step)
    total = acc_ref[:1, :]
    log_ref[0, 0] = jnp.log(total)
    mixed = acc_ref[HD:, :] / total
    rows = [mixed[:, head * length : (head + 1) * length] for head in range(G)]
    out_ref[0] = jnp.concatenate(rows, axis=0).T.astype(out_ref.dtype)


def attend_back_kernel(
    meta_ref,
    start_ref,
    index_ref,
    query_ref,
    kv_ref,
    grad_ref,
    log_ref,
    inner_ref,
    _,
    dq_ref,
    dkv_ref,
    acc_ref,
    rows_ref,
    grad_rows_ref,
):
    length = query_ref.shape[1]
    start, query_index = start_ref[0], index_ref[0]
    turned = meta_ref[pl.program_id(0), 3]
    acc_ref[...] = jnp.zeros_like(acc_ref)
    dkv_ref[...] = jnp.zeros_like(dkv_ref)
    pad_heads(rows_ref, query_ref, 0)
    pad_heads(grad_rows_ref, grad_ref, 1)

    def step(chunk, masked):
        slot = chunk + turned * (kv_ref.shape[0] - 1 - 2 * chunk)
        kv = kv_ref[slot, 0, 0]
        total = jnp.zeros((length, 2 * HD), F32)
        for head in range(G):
            part = pl.ds(head * length, length)
            query, grad = rows_ref[part], grad_rows_ref[part]
            probs = jnp.exp(dot(kv, query, NT) - log_ref[0, 0, :, part])
            if masked:
                mask = chunk_mask(chunk, length, start[:, :length], query_index[:, :length])
                probs = jnp.where(mask, probs, 0.0)
            d_probs = dot(kv, grad, NT)
            d_scores = (probs * (d_probs - inner_ref[0, 0, :, part])).astype(LOW)
            total = total + dot(d_scores, query, NN) + dot(probs.astype(LOW), grad, NN)
            acc_ref[:, part] += dot(kv, d_scores, TN)
        dkv_ref[slot, 0, 0] = total.astype(dkv_ref.dtype)

    for_chunks(meta_ref, step)
    rows = [acc_ref[:HD, head * length : (head + 1) * length] for head in range(G)]
    dq_ref[0] = jnp.concatenate(rows, axis=0).T * (1.0 / math.sqrt(HD))


def attention_specs(n_ctx, length):
    kv = pl.BlockSpec((n_ctx, 1, 1, length, 2 * HD), lambda b, h, *_: (0, b, h, 0, 0))
    row = pl.BlockSpec((1, 1, 1, G * length), lambda b, h, *_: (b, h, 0, 0))
    start = pl.BlockSpec((1, 1, G * length), lambda b, h, *_: (b, 0, 0))
    natural = pl.BlockSpec((1, length, G * HD), lambda b, h, *_: (b, 0, h))
    return kv, row, start, natural


def attend(meta, start, index, query, kv_all):
    n_ctx, blocks, heads, length, _ = kv_all.shape
    kv_spec, row_spec, start_spec, natural = attention_specs(n_ctx, length)
    pairs = blocks * heads * G * length * n_ctx * length
    return pl.pallas_call(
        attend_kernel,
        grid_spec=pltpu.PrefetchScalarGridSpec(
            num_scalar_prefetch=1,
            grid=(blocks, heads),
            in_specs=[start_spec, start_spec, natural, kv_spec],
            out_specs=[natural, row_spec],
            scratch_shapes=[
                pltpu.VMEM((2 * HD, G * length), F32),
                pltpu.VMEM((G * length, 2 * HD), LOW),
            ],
        ),
        out_shape=[
            jax.ShapeDtypeStruct((blocks, length, heads * G * HD), LOW),
            jax.ShapeDtypeStruct((blocks, heads, 1, G * length), F32),
        ],
        compiler_params=pltpu.CompilerParams(vmem_limit_bytes=40 * 2**20),
        cost_estimate=pl.CostEstimate(
            flops=pairs * 32, bytes_accessed=2**20, transcendentals=0
        ),
        name="attend",
    )(meta, start, index, query, kv_all)


def attend_back(meta, start, index, query, kv_all, grad, log_total, inner, other):
    n_ctx, blocks, heads, length, _ = kv_all.shape
    kv_spec, row_spec, start_spec, natural = attention_specs(n_ctx, length)
    pairs = blocks * heads * G * length * n_ctx * length
    return pl.pallas_call(
        attend_back_kernel,
        grid_spec=pltpu.PrefetchScalarGridSpec(
            num_scalar_prefetch=1,
            grid=(blocks, heads),
            in_specs=[start_spec, start_spec, natural, kv_spec, natural, row_spec, row_spec]
            + [pl.BlockSpec(memory_space=pl.ANY)],
            out_specs=[natural, kv_spec],
            scratch_shapes=[
                pltpu.VMEM((2 * HD, G * length), F32),
                pltpu.VMEM((G * length, 2 * HD), LOW),
                pltpu.VMEM((G * length, 2 * HD), LOW),
            ],
        ),
        out_shape=[
            jax.ShapeDtypeStruct((blocks, length, heads * G * HD), F32),
            jax.ShapeDtypeStruct(kv_all.shape, LOW),
        ],
        compiler_params=pltpu.CompilerParams(vmem_limit_bytes=40 * 2**20),
        cost_estimate=pl.CostEstimate(
            flops=pairs * 64, bytes_accessed=2**20, transcendentals=0
        ),
        name="attend_back",
    )(meta, start, index, query, kv_all, grad, log_total, inner, other)


MESH = pl.DeviceIdType.MESH
DMA = pltpu.SemaphoreType.DMA


def flip(rank, shift):
    result, bit = rank, 1
    while bit <= shift:
        if shift & bit:
            result = result + bit - 2 * bit * ((rank // bit) % 2)
        bit *= 2
    return result


class Place:
    def __init__(self, n_dp, n_ctx):
        self.n_dp, self.n_ctx = n_dp, n_ctx
        self.last = n_ctx // 2 - 1
        self.dp, self.ctx = lax.axis_index("dp"), lax.axis_index("ctx")
        self.column, self.core = self.ctx // 2, self.ctx % 2
        self.sibling = (self.dp, self.ctx + 1 - 2 * self.core)
        self.above = (self.dp, self.ctx + 2)
        self.below = (self.dp, self.ctx - 2)
        self.opposite = (self.dp, n_ctx - 1 - self.ctx)

    def peer(self, shift):
        return (flip(self.dp, shift), self.ctx)

    def meet(self, along_dp, along_ctx, across):
        barrier = pltpu.get_barrier_semaphore()

        def greet(device):
            pl.semaphore_signal(barrier, inc=1, device_id=device, device_id_type=MESH)

        count = 0
        if across:
            greet(self.opposite)
            count = 1
        if along_dp:
            for shift in range(1, self.n_dp):
                greet(self.peer(shift))
            count = count + self.n_dp - 1
        if along_ctx:
            greet(self.sibling)
            count = count + 1
            if self.last > 0:
                pl.when(self.column > 0)(lambda: greet(self.below))
                pl.when(self.column < self.last)(lambda: greet(self.above))
                count = count + (self.column + self.last - 1) // self.last
                count = count + (2 * self.last - 1 - self.column) // self.last
        pl.semaphore_wait(barrier, count)


def remote(source, target, send_sem, recv_sem, device):
    return pltpu.make_async_remote_copy(
        src_ref=source,
        dst_ref=target,
        send_sem=send_sem,
        recv_sem=recv_sem,
        device_id=device,
        device_id_type=MESH,
    )


CHUNKS = 2


class GatherDp:
    along_dp, along_ctx, across = True, False, False

    def __init__(self, values, n_dp, n_ctx):
        self.rows = values.shape[0]
        self.operand_spec = pl.BlockSpec(memory_space=pl.ANY)
        self.out_spec = pl.BlockSpec(memory_space=pl.ANY)
        self.out_shape = jax.ShapeDtypeStruct((n_dp, *values.shape), values.dtype)
        self.scratch = [DMA(()), DMA((n_dp, CHUNKS, 2)), DMA((n_dp, CHUNKS, 2))]

    def phases(self, at, own, out, local, send, recv):
        size = self.rows // CHUNKS
        halves = at.n_dp == 4
        direct = (1, 2) if halves else tuple(range(1, at.n_dp))
        mine = pltpu.make_async_copy(own, out.at[0], local)

        def straight(shift, chunk):
            part = pl.ds(chunk * size, size)
            return remote(
                own.at[part],
                out.at[shift, part],
                send.at[shift, chunk, 0],
                recv.at[shift, chunk, 0],
                at.peer(shift),
            )

        def turned(shift, chunk):
            part = pl.ds(chunk * size + (2 - shift) * (size // 2), size // 2)
            return remote(
                out.at[3 - shift, part],
                out.at[3, part],
                send.at[3, chunk, shift - 1],
                recv.at[3, chunk, shift - 1],
                at.peer(shift),
            )

        def begin():
            for chunk in range(CHUNKS):
                for shift in direct:
                    straight(shift, chunk).start()
            mine.start()

        def middle(chunk):
            for shift in direct:
                straight(shift, chunk).wait_recv()
                if halves:
                    turned(3 - shift, chunk).start()

        def end():
            for chunk in range(CHUNKS):
                if halves:
                    for shift in direct:
                        turned(shift, chunk).wait()
                for shift in direct:
                    straight(shift, chunk).wait_send()
            mine.wait()

        return begin, [functools.partial(middle, chunk) for chunk in range(CHUNKS)], end


class SumDp:
    along_dp, along_ctx, across = True, False, False

    def __init__(self, values, n_dp, n_ctx):
        _, self.rows, width = values.shape
        size = self.rows // CHUNKS
        self.operand_spec = pl.BlockSpec(memory_space=pltpu.VMEM)
        self.out_spec = pl.BlockSpec(memory_space=pltpu.VMEM)
        self.out_shape = jax.ShapeDtypeStruct((self.rows, width), F32)
        peers = 2 if n_dp == 4 else n_dp - 1
        self.scratch = [
            pltpu.VMEM((2, CHUNKS, size // 2, width), LOW),
            pltpu.VMEM((2, CHUNKS, size // 2, width), LOW),
            pltpu.VMEM((peers, CHUNKS, 2, size // 2, width), LOW),
            DMA((2, CHUNKS)),
            DMA((2, CHUNKS)),
            DMA((peers, CHUNKS, 2)),
            DMA((peers, CHUNKS, 2)),
        ]

    def phases(self, at, parts, out, arrived, joined, sums, t_send, t_recv, p_send, p_recv):
        size = self.rows // CHUNKS
        half = size // 2
        halves = at.n_dp == 4
        direct = (1, 2) if halves else tuple(range(1, at.n_dp))

        def rows(chunk, which):
            return pl.ds(chunk * size + which * half, half)

        def turning(shift, chunk):
            return remote(
                parts.at[3, rows(chunk, shift - 1)],
                arrived.at[shift - 1, chunk],
                t_send.at[shift - 1, chunk],
                t_recv.at[shift - 1, chunk],
                at.peer(shift),
            )

        def final(shift, chunk, which):
            source = parts.at[shift, rows(chunk, which)]
            if halves and which == 2 - shift:
                source = joined.at[shift - 1, chunk]
            return remote(
                source,
                sums.at[shift - 1, chunk, which],
                p_send.at[shift - 1, chunk, which],
                p_recv.at[shift - 1, chunk, which],
                at.peer(shift),
            )

        def begin():
            for chunk in range(CHUNKS):
                if halves:
                    for shift in direct:
                        turning(shift, chunk).start()
                for shift in direct:
                    for which in (0, 1):
                        if not halves or which != 2 - shift:
                            final(shift, chunk, which).start()

        def middle(chunk):
            for shift in direct if halves else ():
                turning(shift, chunk).wait_recv()
                to = 3 - shift
                mine = parts[to, rows(chunk, shift - 1)].astype(F32)
                came = arrived[shift - 1, chunk].astype(F32)
                joined[to - 1, chunk] = (mine + came).astype(LOW)
                final(to, chunk, shift - 1).start()

        def end():
            for chunk in range(CHUNKS):
                for which in (0, 1):
                    total = parts[0, rows(chunk, which)].astype(F32)
                    for shift in direct:
                        final(shift, chunk, which).wait_recv()
                        total = total + sums[shift - 1, chunk, which].astype(F32)
                    out[rows(chunk, which)] = total
            for chunk in range(CHUNKS):
                for shift in direct:
                    if halves:
                        turning(shift, chunk).wait_send()
                    for which in (0, 1):
                        final(shift, chunk, which).wait_send()

        return begin, [functools.partial(middle, chunk) for chunk in range(CHUNKS)], end


class GatherCtx:
    along_dp, along_ctx, across = False, True, False

    def __init__(self, values, n_dp, n_ctx):
        columns = n_ctx // 2
        self.operand_spec = pl.BlockSpec(memory_space=pl.ANY)
        self.out_spec = pl.BlockSpec(memory_space=pl.ANY)
        self.out_shape = jax.ShapeDtypeStruct((n_ctx, *values.shape), values.dtype)
        self.scratch = [DMA(())] + [DMA((columns,))] * 5

    def phases(self, at, own, out, local, up_send, down_send, recv, sib_send, sib_recv):
        mine = pltpu.make_async_copy(own, out.at[at.ctx], local)

        def travel(column, sem, device):
            ref = out.at[2 * column + at.core]
            source = ref
            return remote(source, ref, sem.at[column], recv.at[column], device)

        def to_sibling(column):
            ref = out.at[2 * column + at.core]
            return remote(ref, ref, sib_send.at[column], sib_recv.at[column], at.sibling)

        def from_sibling(column):
            ref = out.at[2 * column + 1 - at.core]
            remote(ref, ref, sib_send.at[column], sib_recv.at[column], at.sibling).wait_recv()

        def pass_on(column):
            pl.when((column <= at.column) & (at.column < at.last))(
                lambda: travel(column, up_send, at.above).start()
            )
            pl.when((column >= at.column) & (at.column > 0))(
                lambda: travel(column, down_send, at.below).start()
            )
            to_sibling(column).start()

        def begin():
            mine.start()
            mine.wait()
            pass_on(at.column)

        def middle(step):
            def arrive(column):
                travel(column, up_send, at.sibling).wait_recv()
                pass_on(column)

            low, high = at.column - step - 1, at.column + step + 1
            pl.when(low >= 0)(lambda: arrive(low))
            pl.when(high <= at.last)(lambda: arrive(high))

        def end():
            @pl.loop(0, at.last + 1)
            def _(column):
                from_sibling(column)
                to_sibling(column).wait_send()
                pl.when((column <= at.column) & (at.column < at.last))(
                    lambda: travel(column, up_send, at.above).wait_send()
                )
                pl.when((column >= at.column) & (at.column > 0))(
                    lambda: travel(column, down_send, at.below).wait_send()
                )

        return begin, [functools.partial(middle, step) for step in range(at.last)], end


class SumCtx:
    along_dp, along_ctx, across = False, True, False

    def __init__(self, values, n_dp, n_ctx):
        columns = n_ctx // 2
        _, rows, width = values.shape
        self.operand_spec = pl.BlockSpec(memory_space=pltpu.VMEM)
        self.out_spec = pl.BlockSpec(memory_space=pltpu.VMEM)
        self.out_shape = jax.ShapeDtypeStruct((rows, width), F32)
        block = pltpu.VMEM((columns, rows, width), LOW)
        self.scratch = [block] * 4 + [DMA((columns,))] * 6

    def phases(
        self,
        at,
        parts,
        out,
        acc,
        from_sib,
        from_below,
        from_above,
        sib_send,
        sib_recv,
        up_send,
        up_recv,
        down_send,
        down_recv,
    ):
        def to_sibling(column):
            return remote(
                parts.at[2 * column + 1 - at.core],
                from_sib.at[column],
                sib_send.at[column],
                sib_recv.at[column],
                at.sibling,
            )

        def to_above(column):
            return remote(
                acc.at[column],
                from_below.at[column],
                up_send.at[column],
                up_recv.at[column],
                at.above,
            )

        def to_below(column):
            return remote(
                acc.at[column],
                from_above.at[column],
                down_send.at[column],
                down_recv.at[column],
                at.below,
            )

        def farthest_first(count):
            return count // 2 if count % 2 else at.last - count // 2

        def begin():
            for count in range(at.last + 1):
                to_sibling(farthest_first(count)).start()

        def line(column):
            to_sibling(column).wait_recv()
            mine = parts[2 * column + at.core].astype(F32) + from_sib[column].astype(F32)
            acc[column] = mine.astype(LOW)

            def add(came):
                acc[column] = (acc[column].astype(F32) + came[column].astype(F32)).astype(LOW)

            @pl.when(column > at.column)
            def _():
                @pl.when(at.column > 0)
                def _():
                    to_above(column).wait_recv()
                    add(from_below)

                to_above(column).start()

            @pl.when(column < at.column)
            def _():
                @pl.when(at.column < at.last)
                def _():
                    to_below(column).wait_recv()
                    add(from_above)

                to_below(column).start()

        def middle(count):
            line(farthest_first(count))

        def end():
            out[...] = acc[at.column].astype(F32)

            @pl.when(at.column > 0)
            def _():
                to_above(at.column).wait_recv()
                out[...] += from_below[at.column].astype(F32)

            @pl.when(at.column < at.last)
            def _():
                to_below(at.column).wait_recv()
                out[...] += from_above[at.column].astype(F32)

            @pl.loop(0, at.last + 1)
            def _(column):
                to_sibling(column).wait_send()
                pl.when(column > at.column)(lambda: to_above(column).wait_send())
                pl.when(column < at.column)(lambda: to_below(column).wait_send())

        return begin, [functools.partial(middle, step) for step in range(at.last + 1)], end


class Mirror:
    along_dp, along_ctx, across = False, False, True

    def __init__(self, values, n_dp, n_ctx):
        self.operand_spec = pl.BlockSpec(memory_space=pl.ANY)
        self.out_spec = pl.BlockSpec(memory_space=pl.ANY)
        self.out_shape = jax.ShapeDtypeStruct(values.shape, values.dtype)
        self.scratch = [DMA(()), DMA(())]

    def phases(self, at, own, out, send, recv):
        copy = remote(own, out, send, recv, at.opposite)
        return copy.start, [], copy.wait


class ExchangeDp:
    along_dp, along_ctx, across = True, False, False

    def __init__(self, values, n_dp, n_ctx):
        self.operand_spec = pl.BlockSpec(memory_space=pl.ANY)
        self.out_spec = pl.BlockSpec(memory_space=pl.ANY)
        self.out_shape = jax.ShapeDtypeStruct(values.shape, values.dtype)
        self.scratch = [DMA(()), DMA((n_dp,)), DMA((n_dp,))]

    def phases(self, at, blocks, out, local, send, recv):
        mine = pltpu.make_async_copy(blocks.at[at.dp], out.at[at.dp], local)

        def to_peer(shift):
            return remote(
                blocks.at[flip(at.dp, shift)],
                out.at[at.dp],
                send.at[shift],
                recv.at[shift],
                at.peer(shift),
            )

        def from_peer(shift):
            ref = out.at[flip(at.dp, shift)]
            return remote(ref, ref, send.at[shift], recv.at[shift], at.peer(shift))

        def begin():
            for shift in range(1, at.n_dp):
                to_peer(shift).start()
            mine.start()

        def end():
            for shift in range(1, at.n_dp):
                from_peer(shift).wait_recv()
                to_peer(shift).wait_send()
            mine.wait()

        return begin, [], end


def move_kernel(jobs, n_dp, n_ctx, n_others, *refs):
    at = Place(n_dp, n_ctx)
    operands, refs = refs[: len(jobs)], refs[len(jobs) + n_others :]
    outs, refs = refs[: len(jobs)], list(refs[len(jobs) :])
    lists = []
    for job, operand, out in zip(jobs, operands, outs):
        scratch = [refs.pop(0) for _ in job.scratch]
        lists.append(job.phases(at, operand, out, *scratch))
    at.meet(
        any(job.along_dp for job in jobs),
        any(job.along_ctx for job in jobs),
        any(job.across for job in jobs),
    )
    for begin, _, _ in lists:
        begin()
    for count in range(max(len(middles) for _, middles, _ in lists)):
        for _, middles, _ in lists:
            if count < len(middles):
                middles[count]()
    for _, _, end in lists:
        end()


def move(collective_id, name, *kinds_and_values, others=()):
    n_dp, n_ctx = lax.axis_size("dp"), lax.axis_size("ctx")
    jobs = [kind(values, n_dp, n_ctx) for kind, values in kinds_and_values]
    values = [value for _, value in kinds_and_values]
    return pl.pallas_call(
        functools.partial(move_kernel, jobs, n_dp, n_ctx, len(others)),
        out_shape=[job.out_shape for job in jobs],
        in_specs=[job.operand_spec for job in jobs]
        + [pl.BlockSpec(memory_space=pl.ANY)] * len(others),
        out_specs=[job.out_spec for job in jobs],
        scratch_shapes=[piece for job in jobs for piece in job.scratch],
        compiler_params=pltpu.CompilerParams(
            collective_id=collective_id, has_side_effects=True, vmem_limit_bytes=58 * 2**20
        ),
        cost_estimate=pl.CostEstimate(flops=0, bytes_accessed=2**20, transcendentals=0),
        name=name,
    )(*values, *others)


def after(values, other):
    first = lax.slice(other.reshape(-1), (0,), (1,))[0]
    return jnp.where(first != first, jnp.zeros_like(values), values)


def pad_rows(values, rows):
    flat = values.reshape(-1)
    return jnp.pad(flat, (0, rows * 128 - flat.size)).reshape(rows, 128)


def pair_sum(blocks):
    while blocks.shape[0] > 1:
        blocks = blocks[0::2] + blocks[1::2]
    return blocks[0]


def body(
    tokens,
    output_grad,
    segment_ids,
    positions,
    qkv_weight,
    qkv_first,
    qkv_second,
    out_weight,
    out_first,
    out_second,
    gate_up_weight,
    gate_up_first,
    gate_up_second,
    down_weight,
    down_first,
    down_second,
    norm_gains,
    norm_first,
    norm_second,
    head_gains,
    head_first,
    head_second,
):
    n_dp, n_ctx = lax.axis_size("dp"), lax.axis_size("ctx")
    ctx_rank = lax.axis_index("ctx")
    seqs, length, width = tokens.shape
    own = norm_gains.shape[1]
    ff = down_weight.shape[0] * n_dp * n_ctx
    part = ff // n_dp

    kv_heads = KV // n_dp
    heads = kv_heads * G
    each = range(seqs)
    blocks = n_dp * seqs

    def spread_width(values):
        values = values.reshape(-1, n_dp, n_ctx, own).transpose(0, 2, 1, 3)
        return values.reshape(-1, width)

    def restore_width(values):
        values = values.reshape(-1, n_ctx, n_dp, own).transpose(0, 2, 1, 3)
        return values.reshape(-1, width)

    turned = jnp.arange(seqs, dtype=jnp.int32) % 2
    rank_of = ctx_rank + turned * (n_ctx - 1 - 2 * ctx_rank)
    places = jnp.stack([segment_ids, positions], axis=1)

    gain_one, gain_two = norm_gains[0][:, None], norm_gains[1][:, None]
    qkv_low = qkv_weight.astype(LOW).astype(F32)
    gate_up_low = gate_up_weight.astype(LOW).astype(F32)
    qkv_scaled = (qkv_low * gain_one).astype(LOW)
    qkv_blocks = jnp.concatenate(
        [
            block.reshape(own, n_dp, -1).transpose(1, 0, 2)
            for block in jnp.split(qkv_scaled, (H * HD, (H + KV) * HD), axis=1)
        ],
        axis=2,
    )
    qkv_cols = qkv_blocks.shape[2]

    def gather_ctx(values):
        return lax.all_gather(values.reshape(-1, values.shape[-1]), "ctx", axis=0, tiled=True)

    def scatter_ctx(values):
        return lax.psum_scatter(values, "ctx", scatter_dimension=0, tiled=True)

    qkv_mine, places_turned = move(
        1, "exchange_qkv", (ExchangeDp, qkv_blocks), (Mirror, pad_rows(places[1], 8))
    )
    qkv_part = gather_ctx(qkv_mine)
    down_part = gather_ctx(down_weight.astype(LOW))
    gate_up_blocks = (gate_up_low * gain_two).astype(LOW).reshape(own, 2, n_dp, part)
    gate_up_blocks = gate_up_blocks.transpose(2, 0, 1, 3).reshape(n_dp, own, 2 * part)
    places_turned = places_turned.reshape(-1)[: 2 * length].reshape(1, 2, length)
    places_of = jnp.concatenate([places[:1], places_turned], axis=0)

    def normed_rows(values):
        inputs = values.astype(F32)
        scale = rms_scale(inputs)
        return inputs, scale, spread_width((inputs * scale).astype(LOW))

    inputs_first, scale_first, normed = normed_rows(tokens[0])
    normed_first, tokens_turned, places_all = move(
        2,
        "gather_normed",
        (GatherDp, normed),
        (Mirror, tokens[1]),
        (GatherDp, pad_rows(places_of, 32)),
        others=(qkv_mine,),
    )
    inputs_second, scale_second, normed = normed_rows(tokens_turned)
    normed_second, grad_turned, gate_up_mine = move(
        3,
        "gather_normed",
        (GatherDp, normed),
        (Mirror, output_grad[1]),
        (ExchangeDp, gate_up_blocks),
    )
    inputs_of, scale_of = [inputs_first, inputs_second], [scale_first, scale_second]
    normed_of = [
        values.reshape(n_dp * length, width) for values in (normed_first, normed_second)
    ]
    projected_of = [
        dot(normed_of[s], qkv_part, NN).reshape(n_dp, length, qkv_cols) for s in each
    ]
    places_all = places_all.reshape(n_dp, -1)[:, : seqs * 2 * length].reshape(blocks, 2, length)

    projected = jnp.stack(projected_of, axis=1).reshape(blocks, length, qkv_cols)
    query_raw = projected[..., : heads * HD].reshape(blocks, length, heads, HD)
    keys_raw = projected[..., heads * HD : (heads + kv_heads) * HD]
    keys_raw = keys_raw.reshape(blocks, length, kv_heads, HD)
    values = projected[..., (heads + kv_heads) * HD :].astype(LOW)
    values = values.reshape(blocks, length, kv_heads, HD)
    segments, place_ids = places_all[:, 0], places_all[:, 1]
    cosine, sine = rotary_tables(place_ids)
    cosine, sine = cosine[:, :, None, :], sine[:, :, None, :]
    query_scale, keys_scale = rms_scale(query_raw), rms_scale(keys_raw)
    query_rot = rotary(query_raw * query_scale * head_gains[0], cosine, sine).astype(LOW)
    keys_rot = rotary(keys_raw * keys_scale * head_gains[1], cosine, sine).astype(LOW)
    kv = jnp.concatenate([keys_rot, values], axis=-1).transpose(0, 2, 1, 3)
    grads = jnp.concatenate([output_grad[0], grad_turned], axis=0)
    kv_all, grad_all = move(
        4,
        "gather_keys",
        (GatherCtx, kv.reshape(blocks * kv_heads * length, 2 * HD)),
        (GatherDp, grads),
        others=(down_part,),
    )
    out_part = gather_ctx(after(out_weight.astype(LOW), kv_all))
    gate_up_part = gather_ctx(after(gate_up_mine, kv_all))
    kv_all = kv_all.reshape(n_ctx, blocks, kv_heads, length, 2 * HD)
    grad_all = grad_all.reshape(blocks * length, width)
    query = query_rot * LOW(1.0 / math.sqrt(HD))
    query = query.reshape(blocks, length, heads * HD)
    place = jnp.tile(rank_of, n_dp)
    index = place[:, None] * length + jnp.arange(length, dtype=jnp.int32)
    start = jnp.where(segments == 0, 0, index - place_ids)
    full = jnp.minimum((jnp.max(start, axis=1) + length - 1) // length, place)
    low = jnp.minimum(jnp.min(start, axis=1) // length, full)
    meta = jnp.stack([place, low, full, jnp.tile(turned, n_dp)], axis=1)
    item = (
        meta,
        jnp.tile(start[:, None, :], (1, 1, G)),
        jnp.tile(index[:, None, :], (1, 1, G)),
        query,
        kv_all,
    )
    attended, log_total = attend(*item)
    attended = attended.reshape(blocks * length, heads * HD)

    def to_blocks(values):
        return values.astype(LOW).reshape(n_dp, -1, width)

    (mixed,) = move(5, "sum_mixed", (SumDp, to_blocks(dot(attended, out_part, NN))))
    inputs = jnp.concatenate(inputs_of, axis=0)
    middle = inputs + mixed
    scale_two = rms_scale(middle)
    (feed_all,) = move(
        6, "gather_feed", (GatherDp, spread_width((middle * scale_two).astype(LOW)))
    )
    feed_all = feed_all.reshape(blocks * length, width)

    gate = dot(feed_all, gate_up_part[:, :part], NN)
    up = dot(feed_all, gate_up_part[:, part:], NN)
    sigmoid_gate = jax.nn.sigmoid(gate)
    silu_gate = gate * sigmoid_gate
    hidden = (silu_gate * up).astype(LOW)
    d_hidden = dot(grad_all, down_part, NT)
    d_gate = d_hidden * up * sigmoid_gate * (1.0 + gate * (1.0 - sigmoid_gate))
    d_up = d_hidden * silu_gate
    d_gate_up = jnp.concatenate([d_gate.astype(LOW), d_up.astype(LOW)], axis=1)
    gate_up_sum = dot(feed_all, d_gate_up, TN).astype(LOW)
    down_sum = dot(hidden, grad_all, TN).astype(LOW)
    gate_up_grad = scatter_ctx(gate_up_sum)
    (d_feed,) = move(
        7,
        "sum_feed",
        (SumDp, to_blocks(dot(d_gate_up, gate_up_part, NT))),
        others=(gate_up_sum,),
    )
    d_middle = grads.astype(F32) + norm_back(restore_width(d_feed), middle, scale_two)
    d_middle_low = d_middle.astype(LOW)
    (d_middle_all,) = move(8, "gather_middle", (GatherDp, d_middle_low))
    down_scattered = scatter_ctx(after(after(down_sum, d_middle_all), gate_up_grad))
    d_middle_all = d_middle_all.reshape(blocks * length, width)

    d_attended = dot(d_middle_all, after(out_part, gate_up_grad), NT).astype(LOW)
    inner = (
        jnp.sum(
            (d_attended.astype(F32) * attended.astype(F32)).reshape(
                blocks, length, kv_heads, G, HD
            ),
            axis=-1,
        )
        .transpose(0, 2, 3, 1)
        .reshape(blocks, kv_heads, 1, G * length)
    )
    grad_items = d_attended.reshape(blocks, length, heads * HD)
    d_query_rot, d_kv = attend_back(*item, grad_items, log_total, inner, gate_up_grad)
    out_sum = dot(attended, d_middle_all, TN).astype(LOW)
    out_grad = scatter_ctx(after(out_sum, down_scattered))
    result, d_kv, gate_up_grad = move(
        9,
        "sum_keys",
        (SumDp, to_blocks(dot(hidden, down_part, NN))),
        (SumCtx, d_kv.reshape(n_ctx, blocks * kv_heads * length, 2 * HD)),
        (ExchangeDp, gate_up_grad.reshape(n_dp, own, 2 * part)),
        others=(down_scattered,),
    )
    outputs = (middle + result).astype(LOW)
    d_kv = d_kv.reshape(blocks, kv_heads, length, 2 * HD).transpose(0, 2, 1, 3)
    d_query_rot = d_query_rot.reshape(blocks, length, heads, HD)
    d_query_norm = rotary_back(d_query_rot, cosine, sine)
    d_query = norm_back(d_query_norm * head_gains[0], query_raw, query_scale)
    d_keys_norm = rotary_back(d_kv[..., :HD], cosine, sine)
    d_keys = norm_back(d_keys_norm * head_gains[1], keys_raw, keys_scale)
    d_projected = jnp.concatenate(
        [
            d_query.astype(LOW).reshape(blocks, length, heads * HD),
            d_keys.astype(LOW).reshape(blocks, length, kv_heads * HD),
            d_kv[..., HD:].astype(LOW).reshape(blocks, length, kv_heads * HD),
        ],
        axis=2,
    ).reshape(n_dp, seqs, length, qkv_cols)
    head_terms = jnp.stack(
        [
            jnp.sum(d_query_norm * query_raw * query_scale, axis=(0, 1, 2)),
            jnp.sum(d_keys_norm * keys_raw * keys_scale, axis=(0, 1, 2)),
        ]
    )
    d_projected_of = [d_projected[:, s].reshape(n_dp * length, qkv_cols) for s in each]
    qkv_sum = sum(dot(normed_of[s], d_projected_of[s], TN) for s in each).astype(LOW)
    qkv_grad = scatter_ctx(qkv_sum)

    def input_gradient(seq, d_normed):
        d_inputs = norm_back(restore_width(d_normed), inputs_of[seq], scale_of[seq])
        return (d_middle[seq * length : (seq + 1) * length] + d_inputs).astype(LOW)

    d_normed, head_terms, outputs_second = move(
        10,
        "sum_normed",
        (SumDp, to_blocks(dot(d_projected_of[1], qkv_part, NT))),
        (GatherCtx, pad_rows(head_terms, 8)),
        (Mirror, outputs[length:]),
        others=(qkv_sum, out_grad),
    )
    head_terms = jnp.sum(head_terms, axis=0)
    d_normed, head_terms, input_grad_second, qkv_grad = move(
        11,
        "sum_normed",
        (SumDp, to_blocks(dot(d_projected_of[0], qkv_part, NT))),
        (GatherDp, pad_rows(head_terms, 32)),
        (Mirror, input_gradient(1, d_normed)),
        (ExchangeDp, qkv_grad.reshape(n_dp, own, qkv_cols)),
    )
    input_grad_first = input_gradient(0, d_normed)
    head_grad = pair_sum(head_terms)[:1].reshape(2, HD)
    qkv_grad = qkv_grad.astype(F32)
    qkv_grad = jnp.concatenate(
        [
            block.transpose(1, 0, 2).reshape(own, -1)
            for block in jnp.split(qkv_grad, (heads * HD, (heads + kv_heads) * HD), axis=2)
        ],
        axis=1,
    )
    out_grad = out_grad.astype(F32)
    down_grad = down_scattered.astype(F32)
    gate_up_grad = gate_up_grad.reshape(n_dp, own, 2, part).transpose(1, 2, 0, 3)
    gate_up_grad = gate_up_grad.reshape(own, 2 * ff).astype(F32)
    norm_grad = jnp.stack(
        [jnp.sum(qkv_low * qkv_grad, axis=1), jnp.sum(gate_up_low * gate_up_grad, axis=1)]
    )
    qkv_new = adam(qkv_weight, qkv_first, qkv_second, qkv_grad * gain_one, RATE_QKV, DECAY)
    out_new = adam(out_weight, out_first, out_second, out_grad, RATE_OUT, DECAY)
    gate_up_new = adam(
        gate_up_weight,
        gate_up_first,
        gate_up_second,
        gate_up_grad * gain_two,
        RATE_GATE_UP,
        DECAY,
    )
    down_new = adam(down_weight, down_first, down_second, down_grad, RATE_DOWN, DECAY)
    norm_new = adam(norm_gains, norm_first, norm_second, norm_grad, RATE_GAIN, 0.0)
    head_new = adam(head_gains, head_first, head_second, head_grad, RATE_GAIN, 0.0)
    return (
        jnp.stack([outputs[:length], outputs_second]),
        jnp.stack([input_grad_first, input_grad_second]),
        *qkv_new,
        *out_new,
        *gate_up_new,
        *down_new,
        *norm_new,
        *head_new,
    )


def solution(mesh):
    tokens_spec = P("dp", "ctx", None)
    matrix = P(("dp", "ctx"), None)
    gains = P(None, ("dp", "ctx"))
    in_specs = (
        (tokens_spec,) * 2 + (P("dp", "ctx"),) * 2 + (matrix,) * 12 + (gains,) * 3 + (P(),) * 3
    )
    out_specs = (tokens_spec,) * 2 + (matrix,) * 12 + (gains,) * 3 + (P(),) * 3
    return jax.shard_map(body, mesh=mesh, in_specs=in_specs, out_specs=out_specs, check_vma=False)
```
